512 devices in a mesh: tm: 32 (over x, y, core), head: 16 (over z).
Axes of the slice: x: 4, y: 4, z: 16, core: 2. Of those that a mesh axis runs over, the one named last changes fastest.
Arguments:
- queries: bfloat16 [16384, 4096], P('tm', 'head'), may hold values from -40 to 40
- keys: bfloat16 [16384, 4096], P('tm', 'head'), may hold values from -40 to 40
- values: bfloat16 [16384, 4096], P('tm', 'head'), may hold values from -6 to 6
- block_mask: int32 [6, 4, 4], replicated, may hold values from 0 to 1, as said below
- out_weight: bfloat16 [4096, 2560], P('head'), may hold values from -0.09375 to 0.09375
Outputs:
- projected: bfloat16 [16384, 2560], P(('tm', 'head'))
The draws below stay inside these ranges and needn't reach their ends.
Inputs may be any that keep to these rules, and one draw needn't show every extreme that they name: `block_mask`: entry [c, a, b] is 1 where query block a of a frame may see key block b of a frame in distance class c; class 0 is all ones, every class has its diagonal blocks.
All inputs are finite; a program needn't handle non-finite values.
Results may differ from the reference program's by a relative error of at most 0.025.
Values may be sent and summed in bfloat16 or wider, within the bound.
No kernel may reach another device: no remote copies, remote signals or barrier semaphores. Data moves between devices by JAX's collectives and lax.ppermute only.
A program may use at most 64 MiB of HBM per device.

```python
import math
import jax
import jax.numpy as jnp
from jax import lax

HD = 128
HEAD_DEV = 2
HEADS = 32
DOUT = 2560
BLK = 128
FT = 512
NB = 4
FRAMES = 32
LEVELS = 5
TOKENS = 16384


def shared_noise(key):
    first = jax.random.normal(jax.random.fold_in(key, 101), (TOKENS, HEADS * HD), jnp.float32)
    second = jax.random.normal(jax.random.fold_in(key, 102), (TOKENS, HEADS * HD), jnp.float32)
    return (first, second)


def draw_queries(key, part):
    first, second = shared_noise(key)
    result = first
    return jnp.clip(result, -40.0, 40.0).astype(jnp.bfloat16)


def draw_keys(key, part):
    first, second = shared_noise(key)
    result = second
    return jnp.clip(result, -40.0, 40.0).astype(jnp.bfloat16)


def draw_block_mask(key, part):
    key = jax.random.fold_in(key, 5)
    level = jnp.arange(LEVELS + 1, dtype=jnp.int32)[:, None, None]
    across = jnp.arange(NB, dtype=jnp.int32)[None, :, None]
    down = jnp.arange(NB, dtype=jnp.int32)[None, None, :]
    width_band = jnp.maximum(jnp.right_shift(jnp.int32(NB), level), 1)
    banded = jnp.abs(across - down) < width_band
    random_bits = jax.random.randint(key, (LEVELS + 1, NB, NB), 0, 1 << 30, dtype=jnp.int32)
    picked = random_bits % jnp.left_shift(jnp.int32(1), level) == 0
    return (banded | picked).astype(jnp.int32)


def block_scale(rng, dims, cuts, low, largest):
    factor_of, own = 1.0, jax.random.fold_in(rng, 6)
    for dim, parts in cuts:
        draws = jnp.exp(jax.random.uniform(jax.random.fold_in(own, dim), (parts,), jnp.float32, low / len(cuts), largest / len(cuts)))
        factor_of = factor_of * jnp.repeat(draws, dims[dim] // parts).reshape([-1 if axis == dim else 1 for axis in range(len(dims))])
    return factor_of


def bell_draw(key, dims, deviation, bound, shards=(), kind=jnp.bfloat16):
    values = jax.random.normal(key, dims, jnp.float32) * deviation
    if len(shards) > 0:
        values = block_scale(key, dims, shards, -0.22, 0.18) * values
    return jnp.clip(values, min=-bound, max=bound).astype(kind)


def setup_inputs(seed: int = 0) -> dict:
    splits = jax.random.split(jax.random.key(seed), 6)
    return {
        "queries": draw_queries(jax.random.fold_in(splits[5], 71), 0),
        "keys": draw_keys(jax.random.fold_in(splits[5], 71), 0),
        "values": bell_draw(splits[2], (TOKENS, HEADS * HD), 1.0, 6.0, ((0, 32), (1, 16))),
        "block_mask": draw_block_mask(jax.random.fold_in(splits[5], 71), 0),
        "out_weight": bell_draw(splits[4], (HEADS * HD, DOUT), (HEADS * HD) ** -0.5, 0.09375, ((0, 16),)),
    }


def expand_mask(table):
    return jnp.repeat(jnp.repeat(table, BLK, axis=0), BLK, axis=1) > 0

def attend_frame(frame_no, queries, keys, values, masks):
    factor = 1.0 / math.sqrt(HD)
    start_row = (frame_no * FT).astype(jnp.int32)
    query_rows = lax.dynamic_slice_in_dim(queries, start_row, FT, 0)
    pairs = [(0, 0)]
    for level in range(1, LEVELS + 1):
        reach_len = 2 ** (level - 1)
        pairs.append((-reach_len, level))
        pairs.append((reach_len, level))
    key_parts = []
    value_parts = []
    mask_parts = []
    for offset, level in pairs:
        other = frame_no + offset
        present = (other >= 0) & (other < FRAMES)
        clipped = jnp.clip(other, 0, FRAMES - 1)
        other_row = (clipped * FT).astype(jnp.int32)
        key_parts.append(lax.dynamic_slice_in_dim(keys, other_row, FT, 0))
        value_parts.append(lax.dynamic_slice_in_dim(values, other_row, FT, 0))
        mask_parts.append(masks[level] & present)
    key_rows = jnp.concatenate(key_parts, axis=0)
    value_rows = jnp.concatenate(value_parts, axis=0)
    allowed = jnp.concatenate(mask_parts, axis=1)
    query_heads = query_rows.reshape(FT, HEADS, HD).astype(jnp.float32)
    key_heads = key_rows.reshape(-1, HEADS, HD).astype(jnp.float32)
    value_heads = value_rows.reshape(-1, HEADS, HD).astype(jnp.float32)
    scores = jnp.einsum('thd,uhd->htu', query_heads, key_heads) * factor
    scores = jnp.where(allowed[None], scores, jnp.float32(-1e+30))
    peak = lax.optimization_barrier(jnp.max(scores, axis=2, keepdims=True))
    weights = jnp.where(allowed[None], jnp.exp(scores - peak), jnp.float32(0.0))
    denom = lax.optimization_barrier(jnp.sum(weights, axis=2))
    rounded = lax.optimization_barrier(weights.astype(jnp.bfloat16)).astype(jnp.float32)
    summed = jnp.einsum('htu,uhd->thd', rounded, value_heads)
    attended = summed / jnp.transpose(denom)[:, :, None]
    return attended.astype(jnp.bfloat16).reshape(FT, HEADS * HD)

def reference(queries, keys, values, block_mask, out_weight):
    masks = [expand_mask(block_mask[level]) for level in range(LEVELS + 1)]
    frame_ids = jnp.arange(FRAMES, dtype=jnp.int32)
    attended = lax.map(lambda frame_no: attend_frame(frame_no, queries, keys, values, masks), frame_ids)
    attended = attended.reshape(TOKENS, HEADS * HD)
    group_width = HEAD_DEV * HD
    groups = HEADS // HEAD_DEV
    grouped = attended.reshape(TOKENS, groups, group_width)
    weight_groups = out_weight.reshape(groups, group_width, DOUT)

    def add_group(group, total):
        left = lax.dynamic_index_in_dim(grouped, group, axis=1, keepdims=False)
        right = lax.dynamic_index_in_dim(weight_groups, group, axis=0, keepdims=False)
        partial_sum = jnp.dot(left, right, preferred_element_type=jnp.float32).astype(jnp.bfloat16)
        return total + lax.optimization_barrier(partial_sum).astype(jnp.float32)
    total = lax.fori_loop(0, groups, add_group, jnp.zeros((TOKENS, DOUT), jnp.float32))
    return total.astype(jnp.bfloat16)
```

```python
import functools
import math

import jax
import jax.numpy as jnp
from jax import lax
from jax.experimental import pallas as pl
from jax.experimental.pallas import tpu as pltpu
from jax.sharding import PartitionSpec as P

HD = 128
BLK = 128
FT = 512
NB = 4
ROWS = 32
DOUT = 2560
HIDDEN = -1e30
SCALE = math.log2(math.e) / math.sqrt(HD)
VMEM = 40 * 1024 * 1024


def tile_scores(q, kv_ref, frame, bias_ref, base):
    scores = lax.dot_general(
        q, kv_ref[2 * frame], (((1,), (1,)), ((), ())), preferred_element_type=jnp.float32
    )
    return [scores[:, b * BLK : (b + 1) * BLK] + bias_ref[base + b] for b in range(NB)]


def attend_kernel(sources, n_kv, first, last, *refs):
    bias_ref, q_ref = refs[:2]
    kv_refs = refs[2 : 2 + n_kv]
    rest = refs[2 + n_kv :]
    if first:
        outs = rest
    else:
        state_in, outs = rest[:3], rest[3:]

    def tile(step, carry):
        frame = step // NB
        block = step % NB
        rows = pl.ds(pl.multiple_of(block * BLK, BLK), BLK)
        q = q_ref[frame, rows, :]
        pieces = []
        for kv_no, cross, bias_no in sources:
            key_frame = 1 - frame if cross else frame
            base = ((bias_no * 2 + frame) * NB + block) * NB
            pieces.append(tile_scores(q, kv_refs[kv_no], key_frame, bias_ref, base))
        top = functools.reduce(jnp.maximum, [s for piece in pieces for s in piece])
        peak = jnp.max(top, axis=1, keepdims=True)
        if not first:
            old = state_in[0][frame, rows, :]
            peak = jnp.maximum(old, peak)
            shrink = jnp.exp2((old - peak) * SCALE)
            total = state_in[1][frame, rows, :] * shrink
            acc = state_in[2][frame, rows, :] * shrink
        else:
            peak = jnp.broadcast_to(peak, (BLK, BLK))
            total = jnp.zeros((BLK, BLK), jnp.float32)
            acc = jnp.zeros((BLK, HD), jnp.float32)
        for (kv_no, cross, _), piece in zip(sources, pieces):
            key_frame = 1 - frame if cross else frame
            weights = [jnp.exp2((s - peak) * SCALE) for s in piece]
            total = total + sum(weights)
            packed = jnp.concatenate([w.astype(jnp.bfloat16) for w in weights], axis=1)
            acc = acc + jnp.dot(
                packed, kv_refs[kv_no][2 * key_frame + 1], preferred_element_type=jnp.float32
            )
        if last:
            denom = jnp.sum(total, axis=1, keepdims=True)
            attended = (acc / denom).astype(jnp.bfloat16)
            for i in range(BLK // ROWS):
                outs[0][block * (BLK // ROWS) + i, frame] = attended[i * ROWS : (i + 1) * ROWS]
        else:
            outs[0][frame, rows, :] = peak
            outs[1][frame, rows, :] = total
            outs[2][frame, rows, :] = acc
        return carry

    lax.fori_loop(0, 2 * NB, tile, 0)


def attend(bias, q, kvs, sources, state, last):
    first = state is None
    held = jax.ShapeDtypeStruct((2, FT, HD), jnp.float32)
    if last:
        out_shape = (jax.ShapeDtypeStruct((FT // ROWS, 2, ROWS, HD), jnp.bfloat16),)
    else:
        out_shape = (held,) * 3
    vmem = pl.BlockSpec(memory_space=pltpu.VMEM)
    smem = pl.BlockSpec(memory_space=pltpu.SMEM)
    states = () if first else tuple(state)
    pairs = len(sources) * 2
    out = pl.pallas_call(
        functools.partial(attend_kernel, sources, len(kvs), first, last),
        out_shape=out_shape,
        in_specs=[smem] + [vmem] * (1 + len(kvs) + len(states)),
        out_specs=(vmem,) * len(out_shape),
        compiler_params=pltpu.CompilerParams(vmem_limit_bytes=VMEM),
        cost_estimate=pl.CostEstimate(
            flops=pairs * 4 * FT * FT * HD,
            bytes_accessed=len(kvs) * 4 * FT * HD * 2,
            transcendentals=pairs * FT * FT,
        ),
    )(bias, q, *kvs, *states)
    return out[0] if last else out


def project_kernel(place_ref, own_ref, other_ref, w_ref, out_ref, lhs_ref):
    @pl.when(pl.program_id(0) == 0)
    def _():
        for z in range(own_ref.shape[0]):
            cols = slice(z * HD, (z + 1) * HD)
            lhs_ref[: 2 * ROWS, cols] = own_ref[z]
            lhs_ref[2 * ROWS :, cols] = other_ref[z]

    part = jnp.dot(lhs_ref[...], w_ref[...], preferred_element_type=jnp.float32)
    part = part.astype(jnp.bfloat16)
    for k in range(4):
        out_ref[place_ref[k]] = part[k * ROWS : (k + 1) * ROWS]


def project(place, own, other, weight):
    groups = own.shape[0]
    depth, width = weight.shape
    step = 256
    return pl.pallas_call(
        project_kernel,
        grid=(width // step,),
        out_shape=jax.ShapeDtypeStruct((4, ROWS, width), jnp.bfloat16),
        in_specs=[
            pl.BlockSpec(memory_space=pltpu.SMEM),
            pl.BlockSpec((groups, 2 * ROWS, HD), lambda n: (0, 0, 0)),
            pl.BlockSpec((groups, 2 * ROWS, HD), lambda n: (0, 0, 0)),
            pl.BlockSpec((depth, step), lambda n: (0, n)),
        ],
        out_specs=pl.BlockSpec((4, ROWS, step), lambda n: (0, 0, n)),
        scratch_shapes=[pltpu.VMEM((4 * ROWS, depth), jnp.bfloat16)],
        compiler_params=pltpu.CompilerParams(vmem_limit_bytes=VMEM),
        cost_estimate=pl.CostEstimate(
            flops=8 * ROWS * depth * width, bytes_accessed=depth * width * 2, transcendentals=0
        ),
    )(place, own, other, weight)


def add_kernel(in_ref, out_ref):
    half = in_ref.shape[2]
    for p in range(2):
        both = in_ref[2 * p].astype(jnp.float32) + in_ref[2 * p + 1].astype(jnp.float32)
        out_ref[:, p * half : (p + 1) * half] = both.astype(jnp.bfloat16)


def add_cores(parts):
    return pl.pallas_call(
        add_kernel,
        out_shape=jax.ShapeDtypeStruct((ROWS, 2 * parts.shape[2]), jnp.bfloat16),
        in_specs=[pl.BlockSpec(memory_space=pltpu.VMEM)],
        out_specs=pl.BlockSpec(memory_space=pltpu.VMEM),
        compiler_params=pltpu.CompilerParams(vmem_limit_bytes=VMEM),
    )(parts)


def shards(queries, keys, values, block_mask, out_weight):
    me = lax.axis_index("tm")
    core = me % 2
    y = (me // 2) % 4
    x = me // 8
    side = y % 2

    def chips(go):
        pairs = []
        for i in range(32):
            to = go(i // 8, (i // 2) % 4)
            if to is not None:
                pairs.append((i, to[0] * 8 + to[1] * 2 + i % 2))
        return pairs

    def send(array, pairs):
        return lax.ppermute(array, "tm", pairs)

    half = DOUT // 2
    weight = lax.dynamic_slice(out_weight, (core * HD, side * half), (HD, half))
    weight = lax.all_gather(weight, "head", axis=0, tiled=True)

    def split(array):
        low, high = array[:, :HD], array[:, HD:]
        return jnp.where(core == 0, low, high), jnp.where(core == 0, high, low)

    (q_own, q_give), (k_own, k_give), (v_own, v_give) = map(split, (queries, keys, values))
    swap = [(i, i ^ 1) for i in range(32)]
    kv_got = send(jnp.stack([k_give, v_give]), swap)
    q_got = send(q_give, swap)
    local = jnp.concatenate([jnp.stack([k_own, v_own]), kv_got], axis=0)
    q = jnp.stack([q_own, q_got])

    above = send(local, chips(lambda x, y: (x + 1, y) if x < 3 else None))
    below = send(local, chips(lambda x, y: (x - 1, y) if x > 0 else None))
    across = send(local, chips(lambda x, y: (x, y ^ 2)))
    beside = send(local, chips(lambda x, y: (x, y ^ 1)))
    far = send(local, chips(lambda x, y: (x ^ 2, y)))
    turned = jnp.where((y == 1) | (y == 2), local, jnp.where(y == 3, above, below))
    other = send(turned, chips(lambda x, y: (x, 3 - y)))
    across_row = send(jnp.where(y >= 2, above, below), chips(lambda x, y: (x, y ^ 2)))

    always = jnp.array([True, True])
    parity = jnp.stack([core, 1 - core])
    even = y % 2 == 0
    has_above, has_below = x > 0, x < 3
    row_end = jnp.where(y == 0, has_above, jnp.where(y == 3, has_below, True))
    row_cross = jnp.where(y < 2, has_above, has_below)
    upper = parity == 1
    levels = [0, 1, 2, 1, 2, 1, 3, 3, 4, 4, 5]
    valid = [
        always,
        always,
        always,
        jnp.where(even, upper, ~upper),
        always & row_end,
        jnp.where(even, ~upper, upper) & row_end,
        always,
        always & row_cross,
        always & has_above,
        always & has_below,
        always,
    ]
    seen = (block_mask[jnp.array(levels)] > 0)[:, None] & jnp.stack(valid)[:, :, None, None]
    bias = jnp.where(seen, jnp.float32(0.0), jnp.float32(HIDDEN)).reshape(-1)

    state = attend(bias, q, [local], [(0, False, 0), (0, True, 1)], None, False)
    state = attend(
        bias,
        q,
        [beside, across, above, below, far],
        [
            (0, False, 2),
            (0, True, 3),
            (1, False, 6),
            (2, False, 8),
            (3, False, 9),
            (4, False, 10),
        ],
        state,
        False,
    )
    attended = attend(
        bias,
        q,
        [other, across_row],
        [(0, False, 4), (0, True, 5), (1, False, 7)],
        state,
        True,
    )

    rows = lax.all_to_all(
        attended.reshape(FT // ROWS, 2 * ROWS, HD), "head", 0, 0, tiled=True
    )
    partner = send(rows, [(i, i ^ 2) for i in range(32)])
    here = me % 4
    place = jnp.stack([here, here ^ 1, here ^ 2, here ^ 3]).astype(jnp.int32)
    parts = project(place, rows, partner, weight)
    quads = [[4 * j + k for k in range(4)] for j in range(8)]
    parts = lax.all_to_all(parts, "tm", 0, 0, tiled=True, axis_index_groups=quads)
    return add_cores(parts)


def solution(mesh):
    return jax.shard_map(
        shards,
        mesh=mesh,
        in_specs=(P("tm", "head"), P("tm", "head"), P("tm", "head"), P(), P("head", None)),
        out_specs=P(("tm", "head"), None),
        check_vma=False,
    )
```

```python
import functools
import math

import jax
import jax.numpy as jnp
from jax import lax
from jax.experimental import pallas as pl
from jax.experimental.pallas import tpu as pltpu
from jax.sharding import PartitionSpec as P

HD = 128
BLK = 128
FT = 512
NB = 4
ROWS = 32
TILE = 256
DOUT = 2560
HIDDEN = -1e30
SCALE = math.log2(math.e) / math.sqrt(HD)
VMEM = 40 * 1024 * 1024


def attend_kernel(sources, split, n_kv, first, last, *refs):
    info_ref, mask_ref, q_ref = refs[:3]
    kv_refs = refs[3 : 3 + n_kv]
    rest = refs[3 + n_kv :]
    state_in, outs = ((), rest) if first else (rest[:3], rest[3:])
    tiles = FT // TILE
    blocks = TILE // BLK

    def fold(frame, tile, seen):
        rows = pl.ds(pl.multiple_of(tile * TILE, TILE), TILE)
        q = q_ref[frame, rows, :]
        pieces = []
        for kv_no, cross, level, valid in seen:
            key_frame = 1 - frame if cross else frame
            scores = lax.dot_general(
                q,
                kv_refs[kv_no][2 * key_frame],
                (((1,), (1,)), ((), ())),
                preferred_element_type=jnp.float32,
            )
            here = info_ref[valid] > 0
            piece = []
            for a in range(blocks):
                row = []
                for b in range(NB):
                    shown = mask_ref[(level * NB + tile * blocks + a) * NB + b] > 0
                    bias = jnp.where(here & shown, jnp.float32(0.0), jnp.float32(HIDDEN))
                    block = scores[a * BLK : (a + 1) * BLK, b * BLK : (b + 1) * BLK]
                    row.append(block + bias)
                piece.append(row)
            pieces.append(piece)
        peaks, totals, accs, places = [], [], [], []
        for a in range(blocks):
            place = pl.ds(pl.multiple_of(tile * TILE + a * BLK, BLK), BLK)
            top = functools.reduce(jnp.maximum, [s for piece in pieces for s in piece[a]])
            peak = jnp.max(top, axis=1, keepdims=True)
            if first:
                peak = jnp.broadcast_to(peak, (BLK, BLK))
                totals.append(jnp.zeros((BLK, BLK), jnp.float32))
                accs.append(jnp.zeros((BLK, HD), jnp.float32))
            else:
                old = state_in[0][frame, place, :]
                peak = jnp.maximum(old, peak)
                shrink = jnp.exp2((old - peak) * SCALE)
                totals.append(state_in[1][frame, place, :] * shrink)
                accs.append(state_in[2][frame, place, :] * shrink)
            peaks.append(peak)
            places.append(place)
        acc = jnp.concatenate(accs, axis=0)
        for (kv_no, cross, _, _), piece in zip(seen, pieces):
            key_frame = 1 - frame if cross else frame
            packed = []
            for a in range(blocks):
                weights = [jnp.exp2((s - peaks[a]) * SCALE) for s in piece[a]]
                totals[a] = totals[a] + sum(weights)
                packed.append(
                    jnp.concatenate([w.astype(jnp.bfloat16) for w in weights], axis=1)
                )
            acc = acc + jnp.dot(
                jnp.concatenate(packed, axis=0),
                kv_refs[kv_no][2 * key_frame + 1],
                preferred_element_type=jnp.float32,
            )
        for a in range(blocks):
            part = acc[a * BLK : (a + 1) * BLK]
            if last:
                denom = jnp.sum(totals[a], axis=1, keepdims=True)
                attended = (part / denom).astype(jnp.bfloat16)
                chunk = (tile * blocks + a) * (BLK // ROWS)
                for i in range(BLK // ROWS):
                    outs[0][chunk + i, frame] = attended[i * ROWS : (i + 1) * ROWS]
            else:
                outs[0][frame, places[a], :] = peaks[a]
                outs[1][frame, places[a], :] = totals[a]
                outs[2][frame, places[a], :] = part

    if split is None:

        @pl.loop(0, 2 * tiles)
        def _(step):
            fold(step // tiles, step % tiles, sources)

    else:
        favoured = info_ref[split]

        @pl.loop(0, tiles)
        def _(tile):
            fold(favoured, tile, sources)
            fold(1 - favoured, tile, [s for s in sources if not s[1]])


def attend(info, mask, q, kvs, sources, split, state, last):
    first = state is None
    held = jax.ShapeDtypeStruct((2, FT, HD), jnp.float32)
    if last:
        out_shape = (jax.ShapeDtypeStruct((FT // ROWS, 2, ROWS, HD), jnp.bfloat16),)
    else:
        out_shape = (held,) * 3
    vmem = pl.BlockSpec(memory_space=pltpu.VMEM)
    smem = pl.BlockSpec(memory_space=pltpu.SMEM)
    states = () if first else tuple(state)
    pairs = len(sources) * 2 - (split is not None)
    out = pl.pallas_call(
        functools.partial(attend_kernel, sources, split, len(kvs), first, last),
        out_shape=out_shape,
        in_specs=[smem, smem] + [vmem] * (1 + len(kvs) + len(states)),
        out_specs=(vmem,) * len(out_shape),
        compiler_params=pltpu.CompilerParams(vmem_limit_bytes=VMEM),
        cost_estimate=pl.CostEstimate(
            flops=pairs * 4 * FT * FT * HD,
            bytes_accessed=len(kvs) * 4 * FT * HD * 2,
            transcendentals=pairs * FT * FT,
        ),
    )(info, mask, q, *kvs, *states)
    return out[0] if last else out


def trade_kernel(place_ref, q_ref, k_ref, v_ref, w_ref, kv_out, q_out, give_out, w_out, sems):
    core, side = place_ref[0], place_ref[1]
    mine = pl.ds(pl.multiple_of(core * HD, HD), HD)
    yours = pl.ds(pl.multiple_of((1 - core) * HD, HD), HD)
    half = w_out.shape[1]
    columns = pl.ds(pl.multiple_of(side * half, HD), half)
    moves = [
        (k_ref.at[:, yours], give_out.at[0]),
        (v_ref.at[:, yours], give_out.at[1]),
        (q_ref.at[:, yours], give_out.at[2]),
        (k_ref.at[:, mine], kv_out.at[0]),
        (v_ref.at[:, mine], kv_out.at[1]),
        (q_ref.at[:, mine], q_out.at[0]),
        (w_ref.at[mine, columns], w_out),
    ]
    copies = [
        pltpu.make_async_copy(src, dst, sems.at[n]) for n, (src, dst) in enumerate(moves)
    ]
    for copy in copies:
        copy.start()
    for copy in copies:
        copy.wait()


def trade(place, queries, keys, values, out_weight):
    hbm = pl.BlockSpec(memory_space=pl.ANY)
    smem = pl.BlockSpec(memory_space=pltpu.SMEM)
    kind = queries.dtype
    return pl.pallas_call(
        trade_kernel,
        out_shape=(
            jax.ShapeDtypeStruct((4, FT, HD), kind),
            jax.ShapeDtypeStruct((2, FT, HD), kind),
            jax.ShapeDtypeStruct((3, FT, HD), kind),
            jax.ShapeDtypeStruct((HD, DOUT // 2), kind),
        ),
        in_specs=[smem, hbm, hbm, hbm, hbm],
        out_specs=(hbm,) * 4,
        scratch_shapes=[pltpu.SemaphoreType.DMA((7,))],
        compiler_params=pltpu.CompilerParams(vmem_limit_bytes=56 * 1024 * 1024),
    )(place, queries, keys, values, out_weight)


def project_kernel(place_ref, own_ref, other_ref, w_ref, out_ref, lhs_ref):
    @pl.when(pl.program_id(0) == 0)
    def _():
        for z in range(own_ref.shape[0]):
            cols = slice(z * HD, (z + 1) * HD)
            lhs_ref[: 2 * ROWS, cols] = own_ref[z]
            lhs_ref[2 * ROWS :, cols] = other_ref[z]

    part = jnp.dot(lhs_ref[...], w_ref[...], preferred_element_type=jnp.float32)
    part = part.astype(jnp.bfloat16)
    for k in range(4):
        out_ref[place_ref[k]] = part[k * ROWS : (k + 1) * ROWS]


def project(place, own, other, weight):
    groups = own.shape[0]
    depth, width = weight.shape
    step = 256
    return pl.pallas_call(
        project_kernel,
        grid=(width // step,),
        out_shape=jax.ShapeDtypeStruct((4, ROWS, width), jnp.bfloat16),
        in_specs=[
            pl.BlockSpec(memory_space=pltpu.SMEM),
            pl.BlockSpec((groups, 2 * ROWS, HD), lambda n: (0, 0, 0)),
            pl.BlockSpec((groups, 2 * ROWS, HD), lambda n: (0, 0, 0)),
            pl.BlockSpec((depth, step), lambda n: (0, n)),
        ],
        out_specs=pl.BlockSpec((4, ROWS, step), lambda n: (0, 0, n)),
        scratch_shapes=[pltpu.VMEM((4 * ROWS, depth), jnp.bfloat16)],
        compiler_params=pltpu.CompilerParams(vmem_limit_bytes=56 * 1024 * 1024),
        cost_estimate=pl.CostEstimate(
            flops=8 * ROWS * depth * width, bytes_accessed=depth * width * 2, transcendentals=0
        ),
    )(place, own, other, weight)


def add_kernel(in_ref, out_ref):
    half = in_ref.shape[2]
    for p in range(2):
        both = in_ref[2 * p].astype(jnp.float32) + in_ref[2 * p + 1].astype(jnp.float32)
        out_ref[:, p * half : (p + 1) * half] = both.astype(jnp.bfloat16)


def add_cores(parts):
    return pl.pallas_call(
        add_kernel,
        out_shape=jax.ShapeDtypeStruct((ROWS, 2 * parts.shape[2]), jnp.bfloat16),
        in_specs=[pl.BlockSpec(memory_space=pltpu.VMEM)],
        out_specs=pl.BlockSpec(memory_space=pltpu.VMEM),
        compiler_params=pltpu.CompilerParams(vmem_limit_bytes=VMEM),
    )(parts)


def shards(queries, keys, values, block_mask, out_weight):
    me = lax.axis_index("tm")
    core = me % 2
    y = (me // 2) % 4
    x = me // 8
    side = y % 2

    def chips(go):
        pairs = []
        for i in range(32):
            to = go(i // 8, (i // 2) % 4)
            if to is not None:
                pairs.append((i, to[0] * 8 + to[1] * 2 + i % 2))
        return pairs

    def send(array, pairs):
        return lax.ppermute(array, "tm", pairs)

    place = jnp.stack([core, side]).astype(jnp.int32)
    kv_own, q_own, give, weight = trade(place, queries, keys, values, out_weight)
    weight = lax.all_gather(weight, "head", axis=0, tiled=True)
    got = send(give, [(i, i ^ 1) for i in range(32)])
    local = lax.dynamic_update_slice(kv_own, got[:2], (2, 0, 0))
    q = lax.dynamic_update_slice(q_own, got[2:], (1, 0, 0))

    above = send(local, chips(lambda x, y: (x + 1, y) if x < 3 else None))
    across = send(local, chips(lambda x, y: (x, y ^ 2)))
    below = send(local, chips(lambda x, y: (x - 1, y) if x > 0 else None))
    beside = send(local, chips(lambda x, y: (x, y ^ 1)))
    far = send(local, chips(lambda x, y: (x ^ 2, y)))
    turned = jnp.where((y == 1) | (y == 2), local, jnp.where(y == 3, above, below))
    other = send(turned, chips(lambda x, y: (x, 3 - y)))

    def next_row(x, y):
        to = x + 1 if y < 2 else x - 1
        return (to, y) if 0 <= to < 4 else None

    across_row = send(across, chips(next_row))

    odd = y % 2
    has_above, has_below = x > 0, x < 3
    row_end = jnp.where(y == 0, has_above, jnp.where(y == 3, has_below, True))
    row_cross = jnp.where(y < 2, has_above, has_below)
    info = jnp.stack(
        [
            core ^ odd ^ 1,
            core ^ odd,
            jnp.int32(1),
            row_end.astype(jnp.int32),
            row_cross.astype(jnp.int32),
            has_above.astype(jnp.int32),
            has_below.astype(jnp.int32),
        ]
    ).astype(jnp.int32)
    mask = block_mask.reshape(-1)

    state = attend(info, mask, q, [local], [(0, False, 0, 2), (0, True, 1, 2)], None, None, False)
    state = attend(
        info,
        mask,
        q,
        [beside, across, above, below, far],
        [
            (0, False, 2, 2),
            (0, True, 1, 2),
            (1, False, 3, 2),
            (2, False, 4, 5),
            (3, False, 4, 6),
            (4, False, 5, 2),
        ],
        0,
        state,
        False,
    )
    attended = attend(
        info,
        mask,
        q,
        [other, across_row],
        [(0, False, 2, 3), (0, True, 1, 3), (1, False, 3, 4)],
        1,
        state,
        True,
    )

    rows = lax.all_to_all(
        attended.reshape(FT // ROWS, 2 * ROWS, HD), "head", 0, 0, tiled=True
    )
    partner = send(rows, [(i, i ^ 2) for i in range(32)])
    here = me % 4
    place = jnp.stack([here, here ^ 1, here ^ 2, here ^ 3]).astype(jnp.int32)
    parts = project(place, rows, partner, weight)
    quads = [[4 * j + k for k in range(4)] for j in range(8)]
    parts = lax.all_to_all(parts, "tm", 0, 0, tiled=True, axis_index_groups=quads)
    return add_cores(parts)


def solution(mesh):
    return jax.shard_map(
        shards,
        mesh=mesh,
        in_specs=(P("tm", "head"), P("tm", "head"), P("tm", "head"), P(), P("head", None)),
        out_specs=P(("tm", "head"), None),
        check_vma=False,
    )
```

```python
import functools
import math

import jax
import jax.numpy as jnp
from jax import lax
from jax.experimental import pallas as pl
from jax.experimental.pallas import tpu as pltpu
from jax.sharding import PartitionSpec as P

HD = 128
BLK = 128
FT = 512
NB = 4
ROWS = 32
TILE = 256
DOUT = 2560
HIDDEN = -1e30
SCALE = math.log2(math.e) / math.sqrt(HD)
VMEM = 40 * 1024 * 1024


def attend_kernel(sources, split, n_kv, first, last, *refs):
    info_ref, mask_ref, q_ref = refs[:3]
    kv_refs = refs[3 : 3 + n_kv]
    rest = refs[3 + n_kv :]
    state_in, outs = ((), rest) if first else (rest[:3], rest[3:])
    tiles = FT // TILE
    blocks = TILE // BLK

    def fold(frame, tile, seen):
        rows = pl.ds(pl.multiple_of(tile * TILE, TILE), TILE)
        q = q_ref[frame, rows, :]
        pieces = []
        for kv_no, cross, level, valid in seen:
            key_frame = 1 - frame if cross else frame
            scores = lax.dot_general(
                q,
                kv_refs[kv_no][2 * key_frame],
                (((1,), (1,)), ((), ())),
                preferred_element_type=jnp.float32,
            )
            here = info_ref[valid] > 0
            piece = []
            for a in range(blocks):
                row = []
                for b in range(NB):
                    shown = mask_ref[(level * NB + tile * blocks + a) * NB + b] > 0
                    bias = jnp.where(here & shown, jnp.float32(0.0), jnp.float32(HIDDEN))
                    block = scores[a * BLK : (a + 1) * BLK, b * BLK : (b + 1) * BLK]
                    row.append(block + bias)
                piece.append(row)
            pieces.append(piece)
        peaks, totals, accs, places = [], [], [], []
        for a in range(blocks):
            place = pl.ds(pl.multiple_of(tile * TILE + a * BLK, BLK), BLK)
            top = functools.reduce(jnp.maximum, [s for piece in pieces for s in piece[a]])
            peak = jnp.max(top, axis=1, keepdims=True)
            if first:
                peak = jnp.broadcast_to(peak, (BLK, BLK))
                totals.append(jnp.zeros((BLK, BLK), jnp.float32))
                accs.append(jnp.zeros((BLK, HD), jnp.float32))
            else:
                old = state_in[0][frame, place, :]
                peak = jnp.maximum(old, peak)
                shrink = jnp.exp2((old - peak) * SCALE)
                totals.append(state_in[1][frame, place, :] * shrink)
                accs.append(state_in[2][frame, place, :] * shrink)
            peaks.append(peak)
            places.append(place)
        acc = jnp.concatenate(accs, axis=0)
        for (kv_no, cross, _, _), piece in zip(seen, pieces):
            key_frame = 1 - frame if cross else frame
            packed = []
            for a in range(blocks):
                weights = [jnp.exp2((s - peaks[a]) * SCALE) for s in piece[a]]
                totals[a] = totals[a] + sum(weights)
                packed.append(
                    jnp.concatenate([w.astype(jnp.bfloat16) for w in weights], axis=1)
                )
            acc = acc + jnp.dot(
                jnp.concatenate(packed, axis=0),
                kv_refs[kv_no][2 * key_frame + 1],
                preferred_element_type=jnp.float32,
            )
        for a in range(blocks):
            part = acc[a * BLK : (a + 1) * BLK]
            if last:
                denom = jnp.sum(totals[a], axis=1, keepdims=True)
                attended = (part / denom).astype(jnp.bfloat16)
                chunk = (tile * blocks + a) * (BLK // ROWS)
                for i in range(BLK // ROWS):
                    outs[0][chunk + i, frame] = attended[i * ROWS : (i + 1) * ROWS]
            else:
                outs[0][frame, places[a], :] = peaks[a]
                outs[1][frame, places[a], :] = totals[a]
                outs[2][frame, places[a], :] = part

    if split is None:

        @pl.loop(0, 2 * tiles)
        def _(step):
            fold(step // tiles, step % tiles, sources)

    else:
        favoured = info_ref[split]

        @pl.loop(0, tiles)
        def _(tile):
            fold(favoured, tile, sources)
            fold(1 - favoured, tile, [s for s in sources if not s[1]])


def attend(info, mask, q, kvs, sources, split, state, last):
    first = state is None
    held = jax.ShapeDtypeStruct((2, FT, HD), jnp.float32)
    if last:
        out_shape = (jax.ShapeDtypeStruct((FT // ROWS, 2, ROWS, HD), jnp.bfloat16),)
    else:
        out_shape = (held,) * 3
    vmem = pl.BlockSpec(memory_space=pltpu.VMEM)
    smem = pl.BlockSpec(memory_space=pltpu.SMEM)
    states = () if first else tuple(state)
    pairs = len(sources) * 2 - (split is not None)
    out = pl.pallas_call(
        functools.partial(attend_kernel, sources, split, len(kvs), first, last),
        out_shape=out_shape,
        in_specs=[smem, smem] + [vmem] * (1 + len(kvs) + len(states)),
        out_specs=(vmem,) * len(out_shape),
        compiler_params=pltpu.CompilerParams(vmem_limit_bytes=VMEM),
        cost_estimate=pl.CostEstimate(
            flops=pairs * 4 * FT * FT * HD,
            bytes_accessed=len(kvs) * 4 * FT * HD * 2,
            transcendentals=pairs * FT * FT,
        ),
    )(info, mask, q, *kvs, *states)
    return out[0] if last else out


def trade_kernel(place_ref, *refs):
    k_mine, v_mine, q_mine, k_yours, v_yours, q_yours, w_block = refs[:7]
    kv_out, q_out, give_out, w_out = refs[7:]
    kv_out[0] = k_mine[...]
    kv_out[1] = v_mine[...]
    q_out[0] = q_mine[...]
    give_out[0] = k_yours[...]
    give_out[1] = v_yours[...]
    give_out[2] = q_yours[...]
    w_out[...] = w_block[...]


def trade(place, queries, keys, values, out_weight):
    kind = queries.dtype
    half = DOUT // 2
    mine = pl.BlockSpec((FT, HD), lambda n, place: (0, place[0]))
    yours = pl.BlockSpec((FT, HD), lambda n, place: (0, 1 - place[0]))
    return pl.pallas_call(
        trade_kernel,
        out_shape=(
            jax.ShapeDtypeStruct((4, FT, HD), kind),
            jax.ShapeDtypeStruct((2, FT, HD), kind),
            jax.ShapeDtypeStruct((3, FT, HD), kind),
            jax.ShapeDtypeStruct((HD, half), kind),
        ),
        grid_spec=pltpu.PrefetchScalarGridSpec(
            num_scalar_prefetch=1,
            grid=(1,),
            in_specs=[mine] * 3
            + [yours] * 3
            + [pl.BlockSpec((HD, half), lambda n, place: (place[0], place[1]))],
            out_specs=(
                pl.BlockSpec((2, FT, HD), lambda n, place: (0, 0, 0)),
                pl.BlockSpec((1, FT, HD), lambda n, place: (0, 0, 0)),
                pl.BlockSpec((3, FT, HD), lambda n, place: (0, 0, 0)),
                pl.BlockSpec((HD, half), lambda n, place: (0, 0)),
            ),
        ),
        compiler_params=pltpu.CompilerParams(vmem_limit_bytes=56 * 1024 * 1024),
    )(place, keys, values, queries, keys, values, queries, out_weight)


def project_kernel(place_ref, own_ref, other_ref, w_ref, out_ref, acc_ref):
    step = pl.program_id(0)
    rows = [
        jnp.concatenate([ref[z] for z in range(own_ref.shape[0])], axis=1)
        for ref in (own_ref, other_ref)
    ]
    part = jnp.dot(
        jnp.concatenate(rows, axis=0), w_ref[...], preferred_element_type=jnp.float32
    )

    @pl.when(step == 0)
    def _():
        acc_ref[...] = part

    @pl.when(step > 0)
    def _():
        acc_ref[...] += part

    @pl.when(step == pl.num_programs(0) - 1)
    def _():
        for k in range(4):
            out_ref[place_ref[k]] = acc_ref[k * ROWS : (k + 1) * ROWS].astype(jnp.bfloat16)


def project(place, own, other, weight):
    groups = own.shape[0]
    depth, width = weight.shape
    steps = 4
    rows = pl.BlockSpec((groups // steps, 2 * ROWS, HD), lambda n: (n, 0, 0))
    return pl.pallas_call(
        project_kernel,
        grid=(steps,),
        out_shape=jax.ShapeDtypeStruct((4, ROWS, width), jnp.bfloat16),
        in_specs=[
            pl.BlockSpec(memory_space=pltpu.SMEM),
            rows,
            rows,
            pl.BlockSpec((depth // steps, width), lambda n: (n, 0)),
        ],
        out_specs=pl.BlockSpec((4, ROWS, width), lambda n: (0, 0, 0)),
        scratch_shapes=[pltpu.VMEM((4 * ROWS, width), jnp.float32)],
        compiler_params=pltpu.CompilerParams(vmem_limit_bytes=56 * 1024 * 1024),
        cost_estimate=pl.CostEstimate(
            flops=8 * ROWS * depth * width, bytes_accessed=depth * width * 2, transcendentals=0
        ),
    )(place, own, other, weight)


def add_kernel(in_ref, out_ref):
    half = in_ref.shape[2]
    for p in range(2):
        both = in_ref[2 * p].astype(jnp.float32) + in_ref[2 * p + 1].astype(jnp.float32)
        out_ref[:, p * half : (p + 1) * half] = both.astype(jnp.bfloat16)


def add_cores(parts):
    return pl.pallas_call(
        add_kernel,
        out_shape=jax.ShapeDtypeStruct((ROWS, 2 * parts.shape[2]), jnp.bfloat16),
        in_specs=[pl.BlockSpec(memory_space=pltpu.VMEM)],
        out_specs=pl.BlockSpec(memory_space=pltpu.VMEM),
        compiler_params=pltpu.CompilerParams(vmem_limit_bytes=VMEM),
    )(parts)


def shards(queries, keys, values, block_mask, out_weight):
    me = lax.axis_index("tm")
    core = me % 2
    y = (me // 2) % 4
    x = me // 8
    side = y % 2

    def chips(go):
        pairs = []
        for i in range(32):
            to = go(i // 8, (i // 2) % 4)
            if to is not None:
                pairs.append((i, to[0] * 8 + to[1] * 2 + i % 2))
        return pairs

    def send(array, pairs):
        return lax.ppermute(array, "tm", pairs)

    place = jnp.stack([core, side]).astype(jnp.int32)
    kv_own, q_own, give, weight = trade(place, queries, keys, values, out_weight)
    weight = lax.all_gather(weight, "head", axis=0, tiled=True)
    got = send(give, [(i, i ^ 1) for i in range(32)])
    local = lax.dynamic_update_slice(kv_own, got[:2], (2, 0, 0))
    q = lax.dynamic_update_slice(q_own, got[2:], (1, 0, 0))

    above = send(local, chips(lambda x, y: (x + 1, y) if x < 3 else None))
    across = send(local, chips(lambda x, y: (x, y ^ 2)))
    below = send(local, chips(lambda x, y: (x - 1, y) if x > 0 else None))
    beside = send(local, chips(lambda x, y: (x, y ^ 1)))
    far = send(local, chips(lambda x, y: (x ^ 2, y)))
    turned = jnp.where((y == 1) | (y == 2), local, jnp.where(y == 3, above, below))
    other = send(turned, chips(lambda x, y: (x, 3 - y)))

    def next_row(x, y):
        to = x + 1 if y < 2 else x - 1
        return (to, y) if 0 <= to < 4 else None

    across_row = send(across, chips(next_row))

    odd = y % 2
    has_above, has_below = x > 0, x < 3
    row_end = jnp.where(y == 0, has_above, jnp.where(y == 3, has_below, True))
    row_cross = jnp.where(y < 2, has_above, has_below)
    info = jnp.stack(
        [
            core ^ odd ^ 1,
            core ^ odd,
            jnp.int32(1),
            row_end.astype(jnp.int32),
            row_cross.astype(jnp.int32),
            has_above.astype(jnp.int32),
            has_below.astype(jnp.int32),
        ]
    ).astype(jnp.int32)
    mask = block_mask.reshape(-1)

    state = attend(info, mask, q, [local], [(0, False, 0, 2), (0, True, 1, 2)], None, None, False)
    state = attend(
        info,
        mask,
        q,
        [beside, across, above, below, far],
        [
            (0, False, 2, 2),
            (0, True, 1, 2),
            (1, False, 3, 2),
            (2, False, 4, 5),
            (3, False, 4, 6),
            (4, False, 5, 2),
        ],
        0,
        state,
        False,
    )
    attended = attend(
        info,
        mask,
        q,
        [other, across_row],
        [(0, False, 2, 3), (0, True, 1, 3), (1, False, 3, 4)],
        1,
        state,
        True,
    )

    rows = lax.all_to_all(
        attended.reshape(FT // ROWS, 2 * ROWS, HD), "head", 0, 0, tiled=True
    )
    partner = send(rows, [(i, i ^ 2) for i in range(32)])
    here = me % 4
    place = jnp.stack([here, here ^ 1, here ^ 2, here ^ 3]).astype(jnp.int32)
    parts = project(place, rows, partner, weight)
    quads = [[4 * j + k for k in range(4)] for j in range(8)]
    parts = lax.all_to_all(parts, "tm", 0, 0, tiled=True, axis_index_groups=quads)
    return add_cores(parts)


def solution(mesh):
    return jax.shard_map(
        shards,
        mesh=mesh,
        in_specs=(P("tm", "head"), P("tm", "head"), P("tm", "head"), P(), P("head", None)),
        out_specs=P(("tm", "head"), None),
        check_vma=False,
    )
```

```python
import functools
import math

import jax
import jax.numpy as jnp
from jax import lax
from jax.experimental import pallas as pl
from jax.experimental.pallas import tpu as pltpu
from jax.sharding import PartitionSpec as P

HD = 128
BLK = 128
FT = 512
NB = 4
ROWS = 32
TILE = 256
DOUT = 2560
HIDDEN = -1e30
SCALE = math.log2(math.e) / math.sqrt(HD)
VMEM = 40 * 1024 * 1024
WIDE = 56 * 1024 * 1024
QUARTER = DOUT // 4


def attend_kernel(sources, split, n_kv, first, last, *refs):
    info_ref, mask_ref, q_ref = refs[:3]
    kv_refs = refs[3 : 3 + n_kv]
    rest = refs[3 + n_kv :]
    state_in, outs = ((), rest) if first else (rest[:3], rest[3:])
    tiles = FT // TILE
    blocks = TILE // BLK

    def fold(frame, tile, seen):
        rows = pl.ds(pl.multiple_of(tile * TILE, TILE), TILE)
        q = q_ref[frame, rows, :]
        pieces = []
        for kv_no, cross, level, valid in seen:
            key_frame = 1 - frame if cross else frame
            scores = lax.dot_general(
                q,
                kv_refs[kv_no][2 * key_frame],
                (((1,), (1,)), ((), ())),
                preferred_element_type=jnp.float32,
            )
            here = info_ref[valid] > 0
            piece = []
            for a in range(blocks):
                row = []
                for b in range(NB):
                    shown = mask_ref[(level * NB + tile * blocks + a) * NB + b] > 0
                    bias = jnp.where(here & shown, jnp.float32(0.0), jnp.float32(HIDDEN))
                    block = scores[a * BLK : (a + 1) * BLK, b * BLK : (b + 1) * BLK]
                    row.append(block + bias)
                piece.append(row)
            pieces.append(piece)
        peaks, totals, accs, places = [], [], [], []
        for a in range(blocks):
            place = pl.ds(pl.multiple_of(tile * TILE + a * BLK, BLK), BLK)
            top = functools.reduce(jnp.maximum, [s for piece in pieces for s in piece[a]])
            peak = jnp.max(top, axis=1, keepdims=True)
            if first:
                peak = jnp.broadcast_to(peak, (BLK, BLK))
                totals.append(jnp.zeros((BLK, BLK), jnp.float32))
                accs.append(jnp.zeros((BLK, HD), jnp.float32))
            else:
                old = state_in[0][frame, place, :]
                peak = jnp.maximum(old, peak)
                shrink = jnp.exp2((old - peak) * SCALE)
                totals.append(state_in[1][frame, place, :] * shrink)
                accs.append(state_in[2][frame, place, :] * shrink)
            peaks.append(peak)
            places.append(place)
        acc = jnp.concatenate(accs, axis=0)
        for (kv_no, cross, _, _), piece in zip(seen, pieces):
            key_frame = 1 - frame if cross else frame
            packed = []
            for a in range(blocks):
                weights = [jnp.exp2((s - peaks[a]) * SCALE) for s in piece[a]]
                totals[a] = totals[a] + sum(weights)
                packed.append(
                    jnp.concatenate([w.astype(jnp.bfloat16) for w in weights], axis=1)
                )
            acc = acc + jnp.dot(
                jnp.concatenate(packed, axis=0),
                kv_refs[kv_no][2 * key_frame + 1],
                preferred_element_type=jnp.float32,
            )
        for a in range(blocks):
            part = acc[a * BLK : (a + 1) * BLK]
            if last:
                denom = jnp.sum(totals[a], axis=1, keepdims=True)
                attended = (part / denom).astype(jnp.bfloat16)
                chunk = (tile * blocks + a) * (BLK // ROWS)
                for i in range(BLK // ROWS):
                    outs[0][chunk + i, frame] = attended[i * ROWS : (i + 1) * ROWS]
            else:
                outs[0][frame, places[a], :] = peaks[a]
                outs[1][frame, places[a], :] = totals[a]
                outs[2][frame, places[a], :] = part

    if split is None:

        @pl.loop(0, 2 * tiles)
        def _(step):
            fold(step // tiles, step % tiles, sources)

    else:
        favoured = info_ref[split]

        @pl.loop(0, tiles)
        def _(tile):
            fold(favoured, tile, sources)
            fold(1 - favoured, tile, [s for s in sources if not s[1]])


def attend(info, mask, q, kvs, sources, split, state, last):
    first = state is None
    held = jax.ShapeDtypeStruct((2, FT, HD), jnp.float32)
    if last:
        out_shape = (jax.ShapeDtypeStruct((FT // ROWS, 2, ROWS, HD), jnp.bfloat16),)
    else:
        out_shape = (held,) * 3
    vmem = pl.BlockSpec(memory_space=pltpu.VMEM)
    smem = pl.BlockSpec(memory_space=pltpu.SMEM)
    states = () if first else tuple(state)
    pairs = len(sources) * 2 - (split is not None)
    out = pl.pallas_call(
        functools.partial(attend_kernel, sources, split, len(kvs), first, last),
        out_shape=out_shape,
        in_specs=[smem, smem] + [vmem] * (1 + len(kvs) + len(states)),
        out_specs=(vmem,) * len(out_shape),
        compiler_params=pltpu.CompilerParams(vmem_limit_bytes=VMEM),
        cost_estimate=pl.CostEstimate(
            flops=pairs * 4 * FT * FT * HD,
            bytes_accessed=len(kvs) * 4 * FT * HD * 2,
            transcendentals=pairs * FT * FT,
        ),
    )(info, mask, q, *kvs, *states)
    return out[0] if last else out


def pick_kernel(core_ref, *refs):
    ins, outs = list(refs), []
    while ins and len(ins[-1].shape) == 3:
        outs.insert(0, ins.pop())
    places = [(out, n) for out in outs for n in range(out.shape[0])]
    for block, (out, n) in zip(ins, places):
        out[n] = block[...]


def pick(core, arrays, other, sizes):
    maps = [
        (lambda n, core: (0, 1 - core[0])) if other else (lambda n, core: (0, core[0]))
        for _ in arrays
    ]
    return pl.pallas_call(
        pick_kernel,
        out_shape=tuple(
            jax.ShapeDtypeStruct((room, FT, HD), arrays[0].dtype) for _, room in sizes
        ),
        grid_spec=pltpu.PrefetchScalarGridSpec(
            num_scalar_prefetch=1,
            grid=(1,),
            in_specs=[pl.BlockSpec((FT, HD), index) for index in maps],
            out_specs=tuple(
                pl.BlockSpec((used, FT, HD), lambda n, core: (0, 0, 0)) for used, _ in sizes
            ),
        ),
        compiler_params=pltpu.CompilerParams(vmem_limit_bytes=WIDE),
    )(core, *arrays)


def cut_kernel(place_ref, w_ref, out_ref):
    out_ref[...] = w_ref[...]


def cut(place, out_weight):
    return pl.pallas_call(
        cut_kernel,
        out_shape=jax.ShapeDtypeStruct((HD, QUARTER), out_weight.dtype),
        grid_spec=pltpu.PrefetchScalarGridSpec(
            num_scalar_prefetch=1,
            grid=(1,),
            in_specs=[pl.BlockSpec((HD, QUARTER), lambda n, place: (place[0], place[1]))],
            out_specs=pl.BlockSpec((HD, QUARTER), lambda n, place: (0, 0)),
        ),
        compiler_params=pltpu.CompilerParams(vmem_limit_bytes=WIDE),
    )(place, out_weight)


def project_kernel(place_ref, *refs):
    row_refs, (w_ref, out_ref) = refs[:4], refs[4:]
    rows = [
        jnp.concatenate([ref[z] for z in range(ref.shape[0])], axis=1) for ref in row_refs
    ]
    part = jnp.dot(
        jnp.concatenate(rows, axis=0), w_ref[...], preferred_element_type=jnp.float32
    ).astype(jnp.bfloat16)
    for k in range(8):
        out_ref[place_ref[k]] = part[k * ROWS : (k + 1) * ROWS]


def project(place, rows, weight):
    depth, width = weight.shape
    vmem = pl.BlockSpec(memory_space=pltpu.VMEM)
    return pl.pallas_call(
        project_kernel,
        out_shape=jax.ShapeDtypeStruct((8, ROWS, width), jnp.bfloat16),
        in_specs=[pl.BlockSpec(memory_space=pltpu.SMEM)] + [vmem] * 5,
        out_specs=vmem,
        compiler_params=pltpu.CompilerParams(vmem_limit_bytes=VMEM),
        cost_estimate=pl.CostEstimate(
            flops=16 * ROWS * depth * width, bytes_accessed=depth * width * 2, transcendentals=0
        ),
    )(place, *rows, weight)


def add_kernel(in_ref, out_ref):
    width = in_ref.shape[2]
    for p in range(in_ref.shape[0] // 2):
        both = in_ref[2 * p].astype(jnp.float32) + in_ref[2 * p + 1].astype(jnp.float32)
        out_ref[:, p * width : (p + 1) * width] = both.astype(jnp.bfloat16)


def add_cores(parts):
    return pl.pallas_call(
        add_kernel,
        out_shape=jax.ShapeDtypeStruct((ROWS, parts.shape[0] // 2 * parts.shape[2]), parts.dtype),
        in_specs=[pl.BlockSpec(memory_space=pltpu.VMEM)],
        out_specs=pl.BlockSpec(memory_space=pltpu.VMEM),
        compiler_params=pltpu.CompilerParams(vmem_limit_bytes=VMEM),
    )(parts)


def shards(queries, keys, values, block_mask, out_weight):
    me = lax.axis_index("tm")
    core = me & 1
    y = (me >> 1) & 3
    x = me >> 3

    def chips(go):
        pairs = []
        for i in range(32):
            to = go(i // 8, (i // 2) % 4)
            if to is not None and 0 <= to[0] < 4:
                pairs.append((i, to[0] * 8 + to[1] * 2 + i % 2))
        return pairs

    def send(array, pairs):
        return lax.ppermute(array, "tm", pairs)

    at_core = core.reshape(1)
    (give,) = pick(at_core, [keys, values, queries], True, [(3, 3)])
    got = send(give, [(i, i ^ 1) for i in range(32)])
    kv_own, q_own = pick(at_core, [keys, values, queries], False, [(2, 4), (1, 2)])
    weight = cut(jnp.stack([core, y]), out_weight)
    weight = lax.all_gather(weight, "head", axis=0, tiled=True)
    local = lax.dynamic_update_slice(kv_own, got[:2], (2, 0, 0))
    q = lax.dynamic_update_slice(q_own, got[2:], (1, 0, 0))

    def neighbour(x, y):
        chip = 4 * x + y + (1 if y % 2 else -1)
        return (chip // 4, chip % 4) if 0 <= chip < 16 else None

    across = send(local, chips(lambda x, y: (x, y ^ 2)))
    above = send(local, chips(lambda x, y: (x + 1, y)))
    below = send(local, chips(lambda x, y: (x - 1, y)))
    beside = send(local, chips(lambda x, y: (x, y ^ 1)))
    far = send(local, chips(lambda x, y: (x ^ 2, y)))
    other = send(local, chips(neighbour))

    odd = y & 1
    has_above, has_below = x > 0, x < 3
    row_end = jnp.where(y == 0, has_above, jnp.where(y == 3, has_below, True))
    row_cross = jnp.where(y < 2, has_above, has_below)
    info = jnp.stack(
        [
            core ^ odd ^ 1,
            core ^ odd,
            jnp.int32(1),
            row_end.astype(jnp.int32),
            row_cross.astype(jnp.int32),
            has_above.astype(jnp.int32),
            has_below.astype(jnp.int32),
        ]
    ).astype(jnp.int32)
    mask = block_mask.reshape(-1)

    state = attend(info, mask, q, [local], [(0, False, 0, 2), (0, True, 1, 2)], None, None, False)

    across, state = lax.optimization_barrier((across, state))
    across_row = send(across, chips(lambda x, y: (x + 1 if y < 2 else x - 1, y)))

    state = attend(
        info,
        mask,
        q,
        [beside, across, above, below, far],
        [
            (0, False, 2, 2),
            (0, True, 1, 2),
            (1, False, 3, 2),
            (2, False, 4, 5),
            (3, False, 4, 6),
            (4, False, 5, 2),
        ],
        0,
        state,
        False,
    )
    attended = attend(
        info,
        mask,
        q,
        [other, across_row],
        [(0, False, 2, 3), (0, True, 1, 3), (1, False, 3, 4)],
        1,
        state,
        True,
    )

    rows = lax.all_to_all(
        attended.reshape(FT // ROWS, 2 * ROWS, HD), "head", 0, 0, tiled=True
    )
    rows = [rows] + [send(rows, [(i, i ^ (2 * k)) for i in range(32)]) for k in (1, 2, 3)]
    here = me & 7
    place = jnp.stack([here ^ k for k in range(8)])
    parts = project(place, rows, weight)
    rings = [[8 * j + k for k in range(8)] for j in range(4)]
    parts = lax.all_to_all(parts, "tm", 0, 0, tiled=True, axis_index_groups=rings)
    return add_cores(parts)


def solution(mesh):
    return jax.shard_map(
        shards,
        mesh=mesh,
        in_specs=(P("tm", "head"), P("tm", "head"), P("tm", "head"), P(), P("head", None)),
        out_specs=P(("tm", "head"), None),
        check_vma=False,
    )
```

```python
import functools
import math

import jax
import jax.numpy as jnp
from jax import lax
from jax.experimental import pallas as pl
from jax.experimental.pallas import tpu as pltpu
from jax.sharding import PartitionSpec as P

HD = 128
BLK = 128
FT = 512
NB = 4
ROWS = 32
TILE = 256
DOUT = 2560
HIDDEN = -1e30
SCALE = math.log2(math.e) / math.sqrt(HD)
VMEM = 40 * 1024 * 1024
WIDE = 56 * 1024 * 1024
NARROW = 24 * 1024 * 1024


def attend_kernel(sources, split, n_kv, first, last, *refs):
    info_ref, mask_ref, q_ref = refs[:3]
    kv_refs = refs[3 : 3 + n_kv]
    rest = refs[3 + n_kv :]
    state_in, outs = ((), rest) if first else (rest[:3], rest[3:])
    tiles = FT // TILE
    blocks = TILE // BLK

    def fold(frame, tile, seen):
        rows = pl.ds(pl.multiple_of(tile * TILE, TILE), TILE)
        q = q_ref[frame, rows, :]
        pieces = []
        for kv_no, cross, level, valid in seen:
            key_frame = 1 - frame if cross else frame
            scores = lax.dot_general(
                q,
                kv_refs[kv_no][2 * key_frame],
                (((1,), (1,)), ((), ())),
                preferred_element_type=jnp.float32,
            )
            here = info_ref[valid] > 0
            piece = []
            for a in range(blocks):
                row = []
                for b in range(NB):
                    shown = mask_ref[(level * NB + tile * blocks + a) * NB + b] > 0
                    bias = jnp.where(here & shown, jnp.float32(0.0), jnp.float32(HIDDEN))
                    block = scores[a * BLK : (a + 1) * BLK, b * BLK : (b + 1) * BLK]
                    row.append(block + bias)
                piece.append(row)
            pieces.append(piece)
        peaks, totals, accs, places = [], [], [], []
        for a in range(blocks):
            place = pl.ds(pl.multiple_of(tile * TILE + a * BLK, BLK), BLK)
            top = functools.reduce(jnp.maximum, [s for piece in pieces for s in piece[a]])
            peak = jnp.max(top, axis=1, keepdims=True)
            if first:
                peak = jnp.broadcast_to(peak, (BLK, BLK))
                totals.append(jnp.zeros((BLK, BLK), jnp.float32))
                accs.append(jnp.zeros((BLK, HD), jnp.float32))
            else:
                old = state_in[0][frame, place, :]
                peak = jnp.maximum(old, peak)
                shrink = jnp.exp2((old - peak) * SCALE)
                totals.append(state_in[1][frame, place, :] * shrink)
                accs.append(state_in[2][frame, place, :] * shrink)
            peaks.append(peak)
            places.append(place)
        acc = jnp.concatenate(accs, axis=0)
        for (kv_no, cross, _, _), piece in zip(seen, pieces):
            key_frame = 1 - frame if cross else frame
            packed = []
            for a in range(blocks):
                weights = [jnp.exp2((s - peaks[a]) * SCALE) for s in piece[a]]
                totals[a] = totals[a] + sum(weights)
                packed.append(
                    jnp.concatenate([w.astype(jnp.bfloat16) for w in weights], axis=1)
                )
            acc = acc + jnp.dot(
                jnp.concatenate(packed, axis=0),
                kv_refs[kv_no][2 * key_frame + 1],
                preferred_element_type=jnp.float32,
            )
        for a in range(blocks):
            part = acc[a * BLK : (a + 1) * BLK]
            if last:
                denom = jnp.sum(totals[a], axis=1, keepdims=True)
                attended = (part / denom).astype(jnp.bfloat16)
                chunk = (tile * blocks + a) * (BLK // ROWS)
                for i in range(BLK // ROWS):
                    outs[0][chunk + i, frame] = attended[i * ROWS : (i + 1) * ROWS]
            else:
                outs[0][frame, places[a], :] = peaks[a]
                outs[1][frame, places[a], :] = totals[a]
                outs[2][frame, places[a], :] = part

    if split is None:

        @pl.loop(0, 2 * tiles)
        def _(step):
            fold(step // tiles, step % tiles, sources)

    else:
        favoured = info_ref[split]

        @pl.loop(0, tiles)
        def _(tile):
            fold(favoured, tile, sources)
            fold(1 - favoured, tile, [s for s in sources if not s[1]])


def attend(info, mask, q, kvs, sources, split, state, last):
    first = state is None
    held = jax.ShapeDtypeStruct((2, FT, HD), jnp.float32)
    if last:
        out_shape = (jax.ShapeDtypeStruct((FT // ROWS, 2, ROWS, HD), jnp.bfloat16),)
    else:
        out_shape = (held,) * 3
    vmem = pl.BlockSpec(memory_space=pltpu.VMEM)
    smem = pl.BlockSpec(memory_space=pltpu.SMEM)
    states = () if first else tuple(state)
    pairs = len(sources) * 2 - (split is not None)
    out = pl.pallas_call(
        functools.partial(attend_kernel, sources, split, len(kvs), first, last),
        out_shape=out_shape,
        in_specs=[smem, smem] + [vmem] * (1 + len(kvs) + len(states)),
        out_specs=(vmem,) * len(out_shape),
        compiler_params=pltpu.CompilerParams(vmem_limit_bytes=VMEM),
        cost_estimate=pl.CostEstimate(
            flops=pairs * 4 * FT * FT * HD,
            bytes_accessed=len(kvs) * 4 * FT * HD * 2,
            transcendentals=pairs * FT * FT,
        ),
    )(info, mask, q, *kvs, *states)
    return out[0] if last else out


def give_kernel(core_ref, side_ref, k_ref, v_ref, q_ref, w_ref, give_out, w_out):
    give_out[0] = k_ref[...]
    give_out[1] = v_ref[...]
    give_out[2] = q_ref[...]
    w_out[...] = w_ref[...]


def keep_kernel(core_ref, k_ref, v_ref, q_ref, kv_out, q_out):
    kv_out[0] = k_ref[...]
    kv_out[1] = v_ref[...]
    q_out[0] = q_ref[...]


def give(core, side, queries, keys, values, out_weight):
    kind = queries.dtype
    half = DOUT // 2
    yours = pl.BlockSpec((FT, HD), lambda n, core, side: (0, 1 - core[0]))
    return pl.pallas_call(
        give_kernel,
        out_shape=(
            jax.ShapeDtypeStruct((3, FT, HD), kind),
            jax.ShapeDtypeStruct((HD, half), kind),
        ),
        grid_spec=pltpu.PrefetchScalarGridSpec(
            num_scalar_prefetch=2,
            grid=(1,),
            in_specs=[yours] * 3
            + [pl.BlockSpec((HD, half), lambda n, core, side: (core[0], side[0]))],
            out_specs=(
                pl.BlockSpec((3, FT, HD), lambda n, core, side: (0, 0, 0)),
                pl.BlockSpec((HD, half), lambda n, core, side: (0, 0)),
            ),
        ),
        compiler_params=pltpu.CompilerParams(vmem_limit_bytes=WIDE),
    )(core, side, keys, values, queries, out_weight)


def keep(core, queries, keys, values):
    kind = queries.dtype
    mine = pl.BlockSpec((FT, HD), lambda n, core: (0, core[0]))
    return pl.pallas_call(
        keep_kernel,
        out_shape=(
            jax.ShapeDtypeStruct((4, FT, HD), kind),
            jax.ShapeDtypeStruct((2, FT, HD), kind),
        ),
        grid_spec=pltpu.PrefetchScalarGridSpec(
            num_scalar_prefetch=1,
            grid=(1,),
            in_specs=[mine] * 3,
            out_specs=(
                pl.BlockSpec((2, FT, HD), lambda n, core: (0, 0, 0)),
                pl.BlockSpec((1, FT, HD), lambda n, core: (0, 0, 0)),
            ),
        ),
        compiler_params=pltpu.CompilerParams(vmem_limit_bytes=WIDE),
    )(core, keys, values, queries)


def product_kernel(rows_ref, w_ref, mine_ref, yours_ref):
    rows = jnp.concatenate([rows_ref[z] for z in range(rows_ref.shape[0])], axis=1)
    part = jnp.dot(rows, w_ref[...], preferred_element_type=jnp.float32).astype(jnp.bfloat16)
    mine_ref[...] = part[:ROWS]
    yours_ref[...] = part[ROWS:]


def product(rows, weight):
    depth, width = weight.shape
    vmem = pl.BlockSpec(memory_space=pltpu.VMEM)
    part = jax.ShapeDtypeStruct((ROWS, width), rows.dtype)
    return pl.pallas_call(
        product_kernel,
        out_shape=(part, part),
        in_specs=[vmem, vmem],
        out_specs=(vmem, vmem),
        compiler_params=pltpu.CompilerParams(vmem_limit_bytes=NARROW),
        cost_estimate=pl.CostEstimate(
            flops=4 * ROWS * depth * width, bytes_accessed=depth * width * 2, transcendentals=0
        ),
    )(rows, weight)


def add_kernel(side_ref, own_ref, got_ref, far_ref, far_other_ref, out_ref):
    width = own_ref.shape[1]
    side = side_ref[0]

    def add(place, left, right):
        both = left[...].astype(jnp.float32) + right[...].astype(jnp.float32)
        columns = pl.ds(pl.multiple_of(place * width, HD), width)
        out_ref[:, columns] = both.astype(jnp.bfloat16)

    add(side, own_ref, got_ref)
    add(1 - side, far_ref, far_other_ref)


def add_cores(side, own, got, far, far_other):
    vmem = pl.BlockSpec(memory_space=pltpu.VMEM)
    return pl.pallas_call(
        add_kernel,
        out_shape=jax.ShapeDtypeStruct((ROWS, 2 * own.shape[1]), own.dtype),
        in_specs=[pl.BlockSpec(memory_space=pltpu.SMEM)] + [vmem] * 4,
        out_specs=vmem,
        compiler_params=pltpu.CompilerParams(vmem_limit_bytes=NARROW),
    )(side, own, got, far, far_other)


def shards(queries, keys, values, block_mask, out_weight):
    me = lax.axis_index("tm")
    core = me & 1
    y = (me >> 1) & 3
    x = me >> 3

    def chips(go):
        pairs = []
        for i in range(32):
            to = go(i // 8, (i // 2) % 4)
            if to is not None:
                pairs.append((i, to[0] * 8 + to[1] * 2 + i % 2))
        return pairs

    def send(array, pairs):
        return lax.ppermute(array, "tm", pairs)

    at_core, at_side = core.reshape(1), (y & 1).reshape(1)
    given, weight = give(at_core, at_side, queries, keys, values, out_weight)
    weight = lax.all_gather(weight, "head", axis=0, tiled=True)
    swap = [(i, i ^ 1) for i in range(32)]
    got = send(given, swap)
    at_core, _ = lax.optimization_barrier((at_core, given))
    kv_own, q_own = keep(at_core, queries, keys, values)
    local = lax.dynamic_update_slice(kv_own, got[:2], (2, 0, 0))
    q = lax.dynamic_update_slice(q_own, got[2:], (1, 0, 0))

    above = send(local, chips(lambda x, y: (x + 1, y) if x < 3 else None))
    across = send(local, chips(lambda x, y: (x, y ^ 2)))
    below = send(local, chips(lambda x, y: (x - 1, y) if x > 0 else None))
    beside = send(local, chips(lambda x, y: (x, y ^ 1)))
    far = send(local, chips(lambda x, y: (x ^ 2, y)))
    turned = jnp.where((y == 1) | (y == 2), local, jnp.where(y == 3, above, below))
    other = send(turned, chips(lambda x, y: (x, 3 - y)))

    def next_row(x, y):
        to = x + 1 if y < 2 else x - 1
        return (to, y) if 0 <= to < 4 else None

    across_row = send(across, chips(next_row))

    odd = y & 1
    has_above, has_below = x > 0, x < 3
    row_end = jnp.where(y == 0, has_above, jnp.where(y == 3, has_below, True))
    row_cross = jnp.where(y < 2, has_above, has_below)
    info = jnp.stack(
        [
            core ^ odd ^ 1,
            core ^ odd,
            jnp.int32(1),
            row_end.astype(jnp.int32),
            row_cross.astype(jnp.int32),
            has_above.astype(jnp.int32),
            has_below.astype(jnp.int32),
        ]
    ).astype(jnp.int32)
    mask = block_mask.reshape(-1)

    state = attend(info, mask, q, [local], [(0, False, 0, 2), (0, True, 1, 2)], None, None, False)
    state = attend(
        info,
        mask,
        q,
        [beside, across, above, below, far],
        [
            (0, False, 2, 2),
            (0, True, 1, 2),
            (1, False, 3, 2),
            (2, False, 4, 5),
            (3, False, 4, 6),
            (4, False, 5, 2),
        ],
        0,
        state,
        False,
    )
    attended = attend(
        info,
        mask,
        q,
        [other, across_row],
        [(0, False, 2, 3), (0, True, 1, 3), (1, False, 3, 4)],
        1,
        state,
        True,
    )

    rows = lax.all_to_all(
        attended.reshape(FT // ROWS, 2 * ROWS, HD), "head", 0, 0, tiled=True
    )
    pair = [(i, i ^ 2) for i in range(32)]
    partner = send(rows, pair)
    own, yours = product(rows, weight)
    got = send(yours, swap)
    far, far_yours = product(partner, weight)
    far = send(far, pair)
    far_other = send(far_yours, [(i, i ^ 3) for i in range(32)])
    return add_cores(at_side, own, got, far, far_other)


def solution(mesh):
    return jax.shard_map(
        shards,
        mesh=mesh,
        in_specs=(P("tm", "head"), P("tm", "head"), P("tm", "head"), P(), P("head", None)),
        out_specs=P(("tm", "head"), None),
        check_vma=False,
    )
```

```python
import functools
import math

import jax
import jax.numpy as jnp
from jax import lax
from jax.experimental import pallas as pl
from jax.experimental.pallas import tpu as pltpu
from jax.sharding import PartitionSpec as P

HD = 128
BLK = 128
FT = 512
NB = 4
ROWS = 32
TILE = 256
DOUT = 2560
HIDDEN = -1e30
SCALE = math.log2(math.e) / math.sqrt(HD)
VMEM = 40 * 1024 * 1024
NARROW = 24 * 1024 * 1024


def attend_kernel(sources, split, n_kv, first, last, *refs):
    info_ref, mask_ref, q_ref = refs[:3]
    kv_refs = refs[3 : 3 + n_kv]
    rest = refs[3 + n_kv :]
    state_in, outs = ((), rest) if first else (rest[:3], rest[3:])
    tiles = FT // TILE
    blocks = TILE // BLK

    def fold(frame, tile, seen):
        rows = pl.ds(pl.multiple_of(tile * TILE, TILE), TILE)
        q = q_ref[frame, rows, :]
        pieces = []
        for kv_no, cross, level, valid in seen:
            key_frame = 1 - frame if cross else frame
            scores = lax.dot_general(
                q,
                kv_refs[kv_no][2 * key_frame],
                (((1,), (1,)), ((), ())),
                preferred_element_type=jnp.float32,
            )
            here = info_ref[valid] > 0
            piece = []
            for a in range(blocks):
                row = []
                for b in range(NB):
                    shown = mask_ref[tile * blocks + a, b, level] > 0
                    bias = jnp.where(here & shown, jnp.float32(0.0), jnp.float32(HIDDEN))
                    block = scores[a * BLK : (a + 1) * BLK, b * BLK : (b + 1) * BLK]
                    row.append(block + bias)
                piece.append(row)
            pieces.append(piece)
        peaks, totals, accs, places = [], [], [], []
        for a in range(blocks):
            place = pl.ds(pl.multiple_of(tile * TILE + a * BLK, BLK), BLK)
            top = functools.reduce(jnp.maximum, [s for piece in pieces for s in piece[a]])
            peak = jnp.max(top, axis=1, keepdims=True)
            if first:
                peak = jnp.broadcast_to(peak, (BLK, BLK))
                totals.append(jnp.zeros((BLK, BLK), jnp.float32))
                accs.append(jnp.zeros((BLK, HD), jnp.float32))
            else:
                old = state_in[0][frame, place, :]
                peak = jnp.maximum(old, peak)
                shrink = jnp.exp2((old - peak) * SCALE)
                totals.append(state_in[1][frame, place, :] * shrink)
                accs.append(state_in[2][frame, place, :] * shrink)
            peaks.append(peak)
            places.append(place)
        acc = jnp.concatenate(accs, axis=0)
        for (kv_no, cross, _, _), piece in zip(seen, pieces):
            key_frame = 1 - frame if cross else frame
            packed = []
            for a in range(blocks):
                weights = [jnp.exp2((s - peaks[a]) * SCALE) for s in piece[a]]
                totals[a] = totals[a] + sum(weights)
                packed.append(
                    jnp.concatenate([w.astype(jnp.bfloat16) for w in weights], axis=1)
                )
            acc = acc + jnp.dot(
                jnp.concatenate(packed, axis=0),
                kv_refs[kv_no][2 * key_frame + 1],
                preferred_element_type=jnp.float32,
            )
        for a in range(blocks):
            part = acc[a * BLK : (a + 1) * BLK]
            if last:
                denom = jnp.sum(totals[a], axis=1, keepdims=True)
                attended = (part / denom).astype(jnp.bfloat16)
                chunk = (tile * blocks + a) * (BLK // ROWS)
                for i in range(BLK // ROWS):
                    outs[0][chunk + i, frame] = attended[i * ROWS : (i + 1) * ROWS]
            else:
                outs[0][frame, places[a], :] = peaks[a]
                outs[1][frame, places[a], :] = totals[a]
                outs[2][frame, places[a], :] = part

    if split is None:

        @pl.loop(0, 2 * tiles)
        def _(step):
            fold(step // tiles, step % tiles, sources)

    else:
        favoured = info_ref[split]

        @pl.loop(0, tiles)
        def _(tile):
            fold(favoured, tile, sources)
            fold(1 - favoured, tile, [s for s in sources if not s[1]])


def attend(info, mask, q, kvs, sources, split, state, last):
    first = state is None
    held = jax.ShapeDtypeStruct((2, FT, HD), jnp.float32)
    if last:
        out_shape = (jax.ShapeDtypeStruct((FT // ROWS, 2, ROWS, HD), jnp.bfloat16),)
    else:
        out_shape = (held,) * 3
    vmem = pl.BlockSpec(memory_space=pltpu.VMEM)
    smem = pl.BlockSpec(memory_space=pltpu.SMEM)
    states = () if first else tuple(state)
    pairs = len(sources) * 2 - (split is not None)
    out = pl.pallas_call(
        functools.partial(attend_kernel, sources, split, len(kvs), first, last),
        out_shape=out_shape,
        in_specs=[smem, smem] + [vmem] * (1 + len(kvs) + len(states)),
        out_specs=(vmem,) * len(out_shape),
        compiler_params=pltpu.CompilerParams(vmem_limit_bytes=VMEM),
        cost_estimate=pl.CostEstimate(
            flops=pairs * 4 * FT * FT * HD,
            bytes_accessed=len(kvs) * 4 * FT * HD * 2,
            transcendentals=pairs * FT * FT,
        ),
    )(info, mask, q, *kvs, *states)
    return out[0] if last else out


def product_kernel(own_ref, far_ref, w_ref, *out_refs):
    rows = [
        jnp.concatenate([ref[z] for z in range(ref.shape[0])], axis=1)
        for ref in (own_ref, far_ref)
    ]
    total = jnp.dot(
        jnp.concatenate(rows, axis=0), w_ref[...], preferred_element_type=jnp.float32
    ).astype(jnp.bfloat16)
    for k, out in enumerate(out_refs):
        out[...] = total[k * ROWS : (k + 1) * ROWS]


def product(own, far, weight):
    depth, width = weight.shape
    vmem = pl.BlockSpec(memory_space=pltpu.VMEM)
    part = jax.ShapeDtypeStruct((ROWS, width), own.dtype)
    return pl.pallas_call(
        product_kernel,
        out_shape=(part,) * 4,
        in_specs=[vmem] * 3,
        out_specs=(vmem,) * 4,
        compiler_params=pltpu.CompilerParams(vmem_limit_bytes=NARROW),
        cost_estimate=pl.CostEstimate(
            flops=8 * ROWS * depth * width, bytes_accessed=depth * width * 2, transcendentals=0
        ),
    )(own, far, weight)


def add_kernel(side_ref, own_ref, got_ref, far_ref, far_other_ref, out_ref):
    width = own_ref.shape[1]
    side = side_ref[0]

    def add(place, left, right):
        both = left[...].astype(jnp.float32) + right[...].astype(jnp.float32)
        columns = pl.ds(pl.multiple_of(place * width, HD), width)
        out_ref[:, columns] = both.astype(jnp.bfloat16)

    add(side, own_ref, got_ref)
    add(1 - side, far_ref, far_other_ref)


def add_cores(side, own, got, far, far_other):
    vmem = pl.BlockSpec(memory_space=pltpu.VMEM)
    return pl.pallas_call(
        add_kernel,
        out_shape=jax.ShapeDtypeStruct((ROWS, 2 * own.shape[1]), own.dtype),
        in_specs=[pl.BlockSpec(memory_space=pltpu.SMEM)] + [vmem] * 4,
        out_specs=vmem,
        compiler_params=pltpu.CompilerParams(vmem_limit_bytes=NARROW),
    )(side, own, got, far, far_other)


def shards(queries, keys, values, block_mask, out_weight):
    me = lax.axis_index("tm")
    core = me & 1
    y = (me >> 1) & 3
    x = me >> 3

    def chips(go):
        pairs = []
        for i in range(32):
            to = go(i // 8, (i // 2) % 4)
            if to is not None:
                pairs.append((i, to[0] * 8 + to[1] * 2 + i % 2))
        return pairs

    def send(array, pairs):
        return lax.ppermute(array, "tm", pairs)

    half = DOUT // 2
    weight = lax.dynamic_slice(out_weight, (core * HD, (y & 1) * half), (HD, half))
    first_core = core == 0
    weight, first_core = lax.optimization_barrier((weight, first_core))
    weight = lax.all_gather(weight, "head", axis=0, tiled=True)

    def head(array, low):
        return jnp.where(low, array[:, :HD], array[:, HD:])

    swap = [(i, i ^ 1) for i in range(32)]
    given = jnp.stack([head(array, ~first_core) for array in (keys, values, queries)])
    got = send(given, swap)
    first_core, _ = lax.optimization_barrier((first_core, given))
    k_own, v_own, q_own = (head(array, first_core) for array in (keys, values, queries))
    local = jnp.concatenate([jnp.stack([k_own, v_own]), got[:2]], axis=0)
    q = jnp.concatenate([q_own[None], got[2:]], axis=0)

    across = send(local, chips(lambda x, y: (x, y ^ 2)))
    above = send(local, chips(lambda x, y: (x + 1, y) if x < 3 else None))
    below = send(local, chips(lambda x, y: (x - 1, y) if x > 0 else None))
    beside = send(local, chips(lambda x, y: (x, y ^ 1)))
    far = send(local, chips(lambda x, y: (x ^ 2, y)))
    turned = jnp.where((y == 1) | (y == 2), local, jnp.where(y == 3, above, below))
    other = send(turned, chips(lambda x, y: (x, 3 - y)))

    def next_row(x, y):
        to = x + 1 if y < 2 else x - 1
        return (to, y) if 0 <= to < 4 else None

    across_row = send(across, chips(next_row))

    odd = y & 1
    has_above, has_below = x > 0, x < 3
    row_end = jnp.where(y == 0, has_above, jnp.where(y == 3, has_below, True))
    row_cross = jnp.where(y < 2, has_above, has_below)
    info = jnp.stack(
        [
            core ^ odd ^ 1,
            core ^ odd,
            jnp.int32(1),
            row_end.astype(jnp.int32),
            row_cross.astype(jnp.int32),
            has_above.astype(jnp.int32),
            has_below.astype(jnp.int32),
        ]
    ).astype(jnp.int32)
    mask = jnp.transpose(block_mask, (1, 2, 0))

    state = attend(info, mask, q, [local], [(0, False, 0, 2), (0, True, 1, 2)], None, None, False)
    state = attend(
        info,
        mask,
        q,
        [beside, across, above, below, far],
        [
            (0, False, 2, 2),
            (0, True, 1, 2),
            (1, False, 3, 2),
            (2, False, 4, 5),
            (3, False, 4, 6),
            (4, False, 5, 2),
        ],
        0,
        state,
        False,
    )
    attended = attend(
        info,
        mask,
        q,
        [other, across_row],
        [(0, False, 2, 3), (0, True, 1, 3), (1, False, 3, 4)],
        1,
        state,
        True,
    )

    rows = lax.all_to_all(
        attended.reshape(FT // ROWS, 2 * ROWS, HD), "head", 0, 0, tiled=True
    )
    pair = [(i, i ^ 2) for i in range(32)]
    own, yours, far, far_yours = product(rows, send(rows, pair), weight)
    far = send(far, pair)
    far_other = send(far_yours, [(i, i ^ 3) for i in range(32)])
    got = send(yours, swap)
    return add_cores((y & 1).reshape(1), own, got, far, far_other)


def solution(mesh):
    return jax.shard_map(
        shards,
        mesh=mesh,
        in_specs=(P("tm", "head"), P("tm", "head"), P("tm", "head"), P(), P("head", None)),
        out_specs=P(("tm", "head"), None),
        check_vma=False,
    )
```

```python
import functools
import math

import jax
import jax.numpy as jnp
from jax import lax
from jax.experimental import pallas as pl
from jax.experimental.pallas import tpu as pltpu
from jax.sharding import PartitionSpec as P

HD = 128
BLK = 128
FT = 512
NB = 4
ROWS = 32
FRAMES = ("x", "y", "core")
HEADS = ("high", "low")
TILE = 256
CORE = 7
DOUT = 2560
HIDDEN = -1e30
SCALE = math.log2(math.e) / math.sqrt(HD)
VMEM = 40 * 1024 * 1024
NARROW = 24 * 1024 * 1024


def attend_kernel(sources, split, n_kv, first, last, *refs):
    info_ref, mask_ref, q_ref = refs[:3]
    kv_refs = refs[3 : 3 + n_kv]
    rest = refs[3 + n_kv :]
    state_in, outs = ((), rest) if first else (rest[:3], rest[3:])
    tiles = FT // TILE
    blocks = TILE // BLK

    def fold(frame, tile, seen):
        rows = pl.ds(pl.multiple_of(tile * TILE, TILE), TILE)
        q = q_ref[frame, rows, :]
        pieces = []
        for kv_no, cross, level, valid in seen:
            key_frame = 1 - frame if cross else frame
            scores = lax.dot_general(
                q,
                kv_refs[kv_no][2 * key_frame],
                (((1,), (1,)), ((), ())),
                preferred_element_type=jnp.float32,
            )
            here = info_ref[valid] > 0
            piece = []
            for a in range(blocks):
                row = []
                for b in range(NB):
                    shown = mask_ref[tile * blocks + a, b, level] > 0
                    bias = jnp.where(here & shown, jnp.float32(0.0), jnp.float32(HIDDEN))
                    block = scores[a * BLK : (a + 1) * BLK, b * BLK : (b + 1) * BLK]
                    row.append(block + bias)
                piece.append(row)
            pieces.append(piece)
        peaks, totals, accs, places = [], [], [], []
        for a in range(blocks):
            place = pl.ds(pl.multiple_of(tile * TILE + a * BLK, BLK), BLK)
            top = functools.reduce(jnp.maximum, [s for piece in pieces for s in piece[a]])
            peak = jnp.max(top, axis=1, keepdims=True)
            if first:
                peak = jnp.broadcast_to(peak, (BLK, BLK))
                totals.append(jnp.zeros((BLK, BLK), jnp.float32))
                accs.append(jnp.zeros((BLK, HD), jnp.float32))
            else:
                old = state_in[0][frame, place, :]
                peak = jnp.maximum(old, peak)
                shrink = jnp.exp2((old - peak) * SCALE)
                totals.append(state_in[1][frame, place, :] * shrink)
                accs.append(state_in[2][frame, place, :] * shrink)
            peaks.append(peak)
            places.append(place)
        acc = jnp.concatenate(accs, axis=0)
        for (kv_no, cross, _, _), piece in zip(seen, pieces):
            key_frame = 1 - frame if cross else frame
            packed = []
            for a in range(blocks):
                weights = [jnp.exp2((s - peaks[a]) * SCALE) for s in piece[a]]
                totals[a] = totals[a] + sum(weights)
                packed.append(
                    jnp.concatenate([w.astype(jnp.bfloat16) for w in weights], axis=1)
                )
            acc = acc + jnp.dot(
                jnp.concatenate(packed, axis=0),
                kv_refs[kv_no][2 * key_frame + 1],
                preferred_element_type=jnp.float32,
            )
        for a in range(blocks):
            part = acc[a * BLK : (a + 1) * BLK]
            if last:
                denom = jnp.sum(totals[a], axis=1, keepdims=True)
                attended = (part / denom).astype(jnp.bfloat16)
                chunk = (tile * blocks + a) * (BLK // ROWS)
                for i in range(BLK // ROWS):
                    outs[0][frame ^ info_ref[CORE], chunk + i] = attended[
                        i * ROWS : (i + 1) * ROWS
                    ]
            else:
                outs[0][frame, places[a], :] = peaks[a]
                outs[1][frame, places[a], :] = totals[a]
                outs[2][frame, places[a], :] = part

    if split is None:

        @pl.loop(0, 2 * tiles)
        def _(step):
            fold(step // tiles, step % tiles, sources)

    else:
        favoured = info_ref[split]

        @pl.loop(0, tiles)
        def _(tile):
            fold(favoured, tile, sources)
            fold(1 - favoured, tile, [s for s in sources if not s[1]])


def attend(info, mask, q, kvs, sources, split, state, last):
    first = state is None
    held = jax.ShapeDtypeStruct((2, FT, HD), jnp.float32)
    if last:
        out_shape = (jax.ShapeDtypeStruct((2, FT // ROWS, ROWS, HD), jnp.bfloat16),)
    else:
        out_shape = (held,) * 3
    vmem = pl.BlockSpec(memory_space=pltpu.VMEM)
    smem = pl.BlockSpec(memory_space=pltpu.SMEM)
    states = () if first else tuple(state)
    pairs = len(sources) * 2 - (split is not None)
    out = pl.pallas_call(
        functools.partial(attend_kernel, sources, split, len(kvs), first, last),
        out_shape=out_shape,
        in_specs=[smem, smem] + [vmem] * (1 + len(kvs) + len(states)),
        out_specs=(vmem,) * len(out_shape),
        compiler_params=pltpu.CompilerParams(vmem_limit_bytes=VMEM),
        cost_estimate=pl.CostEstimate(
            flops=pairs * 4 * FT * FT * HD,
            bytes_accessed=len(kvs) * 4 * FT * HD * 2,
            transcendentals=pairs * FT * FT,
        ),
    )(info, mask, q, *kvs, *states)
    return out[0] if last else out


def product_kernel(low_ref, rows_ref, w_ref, same_ref, other_ref, part_ref):
    rows = jnp.concatenate([rows_ref[n] for n in range(rows_ref.shape[0])], axis=1)
    part_ref[...] = jnp.dot(rows, w_ref[...], preferred_element_type=jnp.float32).astype(
        jnp.bfloat16
    )
    for k, out in enumerate((same_ref, other_ref)):
        start = pl.multiple_of((low_ref[0] ^ k) * ROWS, ROWS)
        out[...] = part_ref[pl.ds(start, ROWS), :]


def product(low, rows, weight):
    vmem = pl.BlockSpec(memory_space=pltpu.VMEM)
    depth, width = weight.shape
    part = jax.ShapeDtypeStruct((ROWS, width), weight.dtype)
    return pl.pallas_call(
        product_kernel,
        out_shape=(part,) * 2,
        in_specs=[pl.BlockSpec(memory_space=pltpu.SMEM)] + [vmem] * 2,
        out_specs=(vmem,) * 2,
        scratch_shapes=[pltpu.VMEM((2 * ROWS, width), weight.dtype)],
        compiler_params=pltpu.CompilerParams(vmem_limit_bytes=NARROW),
        cost_estimate=pl.CostEstimate(
            flops=4 * ROWS * depth * width, bytes_accessed=depth * width * 2, transcendentals=0
        ),
    )(low, rows, weight)


def add_kernel(side_ref, own_ref, got_ref, far_ref, far_other_ref, out_ref):
    width = own_ref.shape[1]
    side = side_ref[0]

    def add(place, left, right):
        both = left[...].astype(jnp.float32) + right[...].astype(jnp.float32)
        columns = pl.ds(pl.multiple_of(place * width, HD), width)
        out_ref[:, columns] = both.astype(jnp.bfloat16)

    add(side, own_ref, got_ref)
    add(1 - side, far_ref, far_other_ref)


def add_halves(side, own, got, far, far_other):
    vmem = pl.BlockSpec(memory_space=pltpu.VMEM)
    return pl.pallas_call(
        add_kernel,
        out_shape=jax.ShapeDtypeStruct((ROWS, 2 * own.shape[1]), own.dtype),
        in_specs=[pl.BlockSpec(memory_space=pltpu.SMEM)] + [vmem] * 4,
        out_specs=vmem,
        compiler_params=pltpu.CompilerParams(vmem_limit_bytes=NARROW),
    )(side, own, got, far, far_other)


def shards(queries, keys, values, block_mask, out_weight):
    me = lax.axis_index(FRAMES)
    core = me & 1
    y = (me >> 1) & 3
    x = me >> 3

    def chips(go):
        pairs = []
        for i in range(32):
            to = go(i // 8, (i // 2) % 4)
            if to is not None:
                pairs.append((i, to[0] * 8 + to[1] * 2 + i % 2))
        return pairs

    def send(array, pairs):
        return lax.ppermute(array, FRAMES, pairs)

    first_core, first_side = core == 0, (y & 1) == 0

    def corner(row, column):
        return out_weight[row * HD : (row + 1) * HD, column * half : (column + 1) * half]

    half = DOUT // 2
    weight = jnp.where(
        first_core,
        jnp.where(first_side, corner(0, 0), corner(0, 1)),
        jnp.where(first_side, corner(1, 0), corner(1, 1)),
    )
    weight, first_core = lax.optimization_barrier((weight, first_core))
    weight = lax.all_gather(weight, ("core", "high"), axis=0, tiled=True)

    def head(array, low):
        return jnp.where(low, array[:, :HD], array[:, HD:])

    swap = [(i, i ^ 1) for i in range(32)]
    given = jnp.stack([head(array, ~first_core) for array in (keys, values, queries)])
    got = send(given, swap)
    first_core, _ = lax.optimization_barrier((first_core, given))
    k_own, v_own, q_own = (head(array, first_core) for array in (keys, values, queries))
    local = jnp.concatenate([jnp.stack([k_own, v_own]), got[:2]], axis=0)
    q = jnp.concatenate([q_own[None], got[2:]], axis=0)

    across = send(local, chips(lambda x, y: (x, y ^ 2)))
    above = send(local, chips(lambda x, y: (x + 1, y) if x < 3 else None))
    below = send(local, chips(lambda x, y: (x - 1, y) if x > 0 else None))
    beside = send(local, chips(lambda x, y: (x, y ^ 1)))
    far = send(local, chips(lambda x, y: (x ^ 2, y)))
    turned = jnp.where((y == 1) | (y == 2), local, jnp.where(y == 3, above, below))
    other = send(turned, chips(lambda x, y: (x, 3 - y)))

    def next_row(x, y):
        to = x + 1 if y < 2 else x - 1
        return (to, y) if 0 <= to < 4 else None

    across_row = send(across, chips(next_row))

    odd = y & 1
    has_above, has_below = x > 0, x < 3
    row_end = jnp.where(y == 0, has_above, jnp.where(y == 3, has_below, True))
    row_cross = jnp.where(y < 2, has_above, has_below)
    info = jnp.stack(
        [
            core ^ odd ^ 1,
            core ^ odd,
            jnp.int32(1),
            row_end.astype(jnp.int32),
            row_cross.astype(jnp.int32),
            has_above.astype(jnp.int32),
            has_below.astype(jnp.int32),
            core,
        ]
    ).astype(jnp.int32)
    mask = jnp.transpose(block_mask, (1, 2, 0))

    state = attend(info, mask, q, [local], [(0, False, 0, 2), (0, True, 1, 2)], None, None, False)
    state = attend(
        info,
        mask,
        q,
        [beside, across, above, below, far],
        [
            (0, False, 2, 2),
            (0, True, 1, 2),
            (1, False, 3, 2),
            (2, False, 4, 5),
            (3, False, 4, 6),
            (4, False, 5, 2),
        ],
        0,
        state,
        False,
    )
    attended = attend(
        info,
        mask,
        q,
        [other, across_row],
        [(0, False, 2, 3), (0, True, 1, 3), (1, False, 3, 4)],
        1,
        state,
        True,
    )

    rows = lax.all_to_all(
        attended.reshape(FT // ROWS, 2 * ROWS, HD), ("core", "high"), 0, 0, tiled=True
    )
    pair = [(i, i ^ 2) for i in range(32)]
    low = lax.axis_index("low").reshape(1)
    far_rows = send(rows, pair)
    own, beside_z = product(low, rows, weight)
    got = lax.ppermute(beside_z, "low", [(0, 1), (1, 0)])
    far_rows, own = lax.optimization_barrier((far_rows, own))
    far, far_beside = product(low, far_rows, weight)
    far, got = lax.optimization_barrier((far, got))
    got_far = send(far, pair)
    both = [(2 * i + k, 2 * (i ^ 2) + (k ^ 1)) for i in range(32) for k in range(2)]
    got_far_other = lax.ppermute(far_beside, FRAMES + ("low",), both)
    return add_halves((y & 1).reshape(1), own, got, got_far, got_far_other)


def solution(mesh):
    devices = mesh.devices.reshape(4, 4, 2, 8, 2)
    mesh = jax.sharding.Mesh(devices, FRAMES + HEADS)
    split = P(FRAMES, HEADS)
    return jax.shard_map(
        shards,
        mesh=mesh,
        in_specs=(split, split, split, P(), P(HEADS, None)),
        out_specs=P(FRAMES + HEADS, None),
        check_vma=False,
    )
```

```python
import functools
import math

import jax
import jax.numpy as jnp
from jax import lax
from jax.experimental import pallas as pl
from jax.experimental.pallas import tpu as pltpu
from jax.sharding import PartitionSpec as P

HD = 128
BLK = 128
FT = 512
NB = 4
ROWS = 32
FRAMES = ("x", "y", "core")
HEADS = ("high", "low")
TILE = 256
CORE = 7
DOUT = 2560
HIDDEN = -1e30
SCALE = math.log2(math.e) / math.sqrt(HD)
VMEM = 40 * 1024 * 1024
NARROW = 24 * 1024 * 1024


def attend_kernel(sources, split, n_kv, first, last, *refs):
    info_ref, mask_ref, q_ref = refs[:3]
    kv_refs = refs[3 : 3 + n_kv]
    rest = refs[3 + n_kv :]
    state_in, outs = ((), rest) if first else (rest[:3], rest[3:])
    tiles = FT // TILE
    blocks = TILE // BLK

    def fold(frame, tile, seen):
        rows = pl.ds(pl.multiple_of(tile * TILE, TILE), TILE)
        q = q_ref[frame, rows, :]
        pieces = []
        for kv_no, cross, level, valid in seen:
            key_frame = 1 - frame if cross else frame
            scores = lax.dot_general(
                q,
                kv_refs[kv_no][2 * key_frame],
                (((1,), (1,)), ((), ())),
                preferred_element_type=jnp.float32,
            )
            here = info_ref[valid] > 0
            piece = []
            for a in range(blocks):
                row = []
                for b in range(NB):
                    shown = mask_ref[tile * blocks + a, b, level] > 0
                    bias = jnp.where(here & shown, jnp.float32(0.0), jnp.float32(HIDDEN))
                    block = scores[a * BLK : (a + 1) * BLK, b * BLK : (b + 1) * BLK]
                    row.append(block + bias)
                piece.append(row)
            pieces.append(piece)
        peaks, totals, accs, places = [], [], [], []
        for a in range(blocks):
            place = pl.ds(pl.multiple_of(tile * TILE + a * BLK, BLK), BLK)
            top = functools.reduce(jnp.maximum, [s for piece in pieces for s in piece[a]])
            peak = jnp.max(top, axis=1, keepdims=True)
            if first:
                peak = jnp.broadcast_to(peak, (BLK, BLK))
                totals.append(jnp.zeros((BLK, BLK), jnp.float32))
                accs.append(jnp.zeros((BLK, HD), jnp.float32))
            else:
                old = state_in[0][frame, place, :]
                peak = jnp.maximum(old, peak)
                shrink = jnp.exp2((old - peak) * SCALE)
                totals.append(state_in[1][frame, place, :] * shrink)
                accs.append(state_in[2][frame, place, :] * shrink)
            peaks.append(peak)
            places.append(place)
        acc = jnp.concatenate(accs, axis=0)
        for (kv_no, cross, _, _), piece in zip(seen, pieces):
            key_frame = 1 - frame if cross else frame
            packed = []
            for a in range(blocks):
                weights = [jnp.exp2((s - peaks[a]) * SCALE) for s in piece[a]]
                totals[a] = totals[a] + sum(weights)
                packed.append(
                    jnp.concatenate([w.astype(jnp.bfloat16) for w in weights], axis=1)
                )
            acc = acc + jnp.dot(
                jnp.concatenate(packed, axis=0),
                kv_refs[kv_no][2 * key_frame + 1],
                preferred_element_type=jnp.float32,
            )
        for a in range(blocks):
            part = acc[a * BLK : (a + 1) * BLK]
            if last:
                denom = jnp.sum(totals[a], axis=1, keepdims=True)
                attended = (part / denom).astype(jnp.bfloat16)
                chunk = (tile * blocks + a) * (BLK // ROWS)
                for i in range(BLK // ROWS):
                    outs[0][frame ^ info_ref[CORE], chunk + i] = attended[
                        i * ROWS : (i + 1) * ROWS
                    ]
            else:
                outs[0][frame, places[a], :] = peaks[a]
                outs[1][frame, places[a], :] = totals[a]
                outs[2][frame, places[a], :] = part

    if split is None:

        @pl.loop(0, 2 * tiles)
        def _(step):
            fold(step // tiles, step % tiles, sources)

    else:
        favoured = info_ref[split]

        @pl.loop(0, tiles)
        def _(tile):
            fold(favoured, tile, sources)
            fold(1 - favoured, tile, [s for s in sources if not s[1]])


def attend(info, mask, q, kvs, sources, split, state, last):
    first = state is None
    held = jax.ShapeDtypeStruct((2, FT, HD), jnp.float32)
    if last:
        out_shape = (jax.ShapeDtypeStruct((2, FT // ROWS, ROWS, HD), jnp.bfloat16),)
    else:
        out_shape = (held,) * 3
    vmem = pl.BlockSpec(memory_space=pltpu.VMEM)
    smem = pl.BlockSpec(memory_space=pltpu.SMEM)
    states = () if first else tuple(state)
    pairs = len(sources) * 2 - (split is not None)
    out = pl.pallas_call(
        functools.partial(attend_kernel, sources, split, len(kvs), first, last),
        out_shape=out_shape,
        in_specs=[smem, smem] + [vmem] * (1 + len(kvs) + len(states)),
        out_specs=(vmem,) * len(out_shape),
        compiler_params=pltpu.CompilerParams(vmem_limit_bytes=VMEM),
        cost_estimate=pl.CostEstimate(
            flops=pairs * 4 * FT * FT * HD,
            bytes_accessed=len(kvs) * 4 * FT * HD * 2,
            transcendentals=pairs * FT * FT,
        ),
    )(info, mask, q, *kvs, *states)
    return out[0] if last else out


def product_kernel(low_ref, rows_ref, w_ref, same_ref, other_ref, part_ref):
    rows = jnp.concatenate([rows_ref[n] for n in range(rows_ref.shape[0])], axis=1)
    part_ref[...] = jnp.dot(rows, w_ref[...], preferred_element_type=jnp.float32).astype(
        jnp.bfloat16
    )
    for k, out in enumerate((same_ref, other_ref)):
        start = pl.multiple_of((low_ref[0] ^ k) * ROWS, ROWS)
        out[...] = part_ref[pl.ds(start, ROWS), :]


def product(low, rows, weight):
    vmem = pl.BlockSpec(memory_space=pltpu.VMEM)
    depth, width = weight.shape
    part = jax.ShapeDtypeStruct((ROWS, width), weight.dtype)
    return pl.pallas_call(
        product_kernel,
        out_shape=(part,) * 2,
        in_specs=[pl.BlockSpec(memory_space=pltpu.SMEM)] + [vmem] * 2,
        out_specs=(vmem,) * 2,
        scratch_shapes=[pltpu.VMEM((2 * ROWS, width), weight.dtype)],
        compiler_params=pltpu.CompilerParams(vmem_limit_bytes=NARROW),
        cost_estimate=pl.CostEstimate(
            flops=4 * ROWS * depth * width, bytes_accessed=depth * width * 2, transcendentals=0
        ),
    )(low, rows, weight)


def add_kernel(side_ref, own_ref, got_ref, far_ref, far_other_ref, out_ref):
    width = own_ref.shape[1]
    side = side_ref[0]

    def add(place, left, right):
        both = left[...].astype(jnp.float32) + right[...].astype(jnp.float32)
        columns = pl.ds(pl.multiple_of(place * width, HD), width)
        out_ref[:, columns] = both.astype(jnp.bfloat16)

    add(side, own_ref, got_ref)
    add(1 - side, far_ref, far_other_ref)


def add_halves(side, own, got, far, far_other):
    vmem = pl.BlockSpec(memory_space=pltpu.VMEM)
    return pl.pallas_call(
        add_kernel,
        out_shape=jax.ShapeDtypeStruct((ROWS, 2 * own.shape[1]), own.dtype),
        in_specs=[pl.BlockSpec(memory_space=pltpu.SMEM)] + [vmem] * 4,
        out_specs=vmem,
        compiler_params=pltpu.CompilerParams(vmem_limit_bytes=NARROW),
    )(side, own, got, far, far_other)


def shards(queries, keys, values, block_mask, out_weight):
    me = lax.axis_index(FRAMES)
    core = me & 1
    y = (me >> 1) & 3
    x = me >> 3

    def chips(go):
        pairs = []
        for i in range(32):
            to = go(i // 8, (i // 2) % 4)
            if to is not None:
                pairs.append((i, to[0] * 8 + to[1] * 2 + i % 2))
        return pairs

    def send(array, pairs):
        return lax.ppermute(array, FRAMES, pairs)

    first_core, first_side = core == 0, (y & 1) == 0

    def corner(row, column):
        return out_weight[row * HD : (row + 1) * HD, column * half : (column + 1) * half]

    half = DOUT // 2
    weight = jnp.where(
        first_core,
        jnp.where(first_side, corner(0, 0), corner(0, 1)),
        jnp.where(first_side, corner(1, 0), corner(1, 1)),
    )
    weight, first_core = lax.optimization_barrier((weight, first_core))
    weight = lax.all_gather(weight, ("core", "high"), axis=0, tiled=True)

    def head(array, low):
        return jnp.where(low, array[:, :HD], array[:, HD:])

    swap = [(i, i ^ 1) for i in range(32)]
    given = jnp.stack([head(array, ~first_core) for array in (keys, values, queries)])
    got = send(given, swap)
    first_core, _ = lax.optimization_barrier((first_core, given))
    k_own, v_own, q_own = (head(array, first_core) for array in (keys, values, queries))
    local = jnp.concatenate([jnp.stack([k_own, v_own]), got[:2]], axis=0)
    q = jnp.concatenate([q_own[None], got[2:]], axis=0)

    across = send(local, chips(lambda x, y: (x, y ^ 2)))
    above = send(local, chips(lambda x, y: (x + 1, y) if x < 3 else None))
    below = send(local, chips(lambda x, y: (x - 1, y) if x > 0 else None))
    beside = send(local, chips(lambda x, y: (x, y ^ 1)))
    far = send(local, chips(lambda x, y: (x ^ 2, y)))
    turned = jnp.where((y == 1) | (y == 2), local, jnp.where(y == 3, above, below))
    other = send(turned, chips(lambda x, y: (x, 3 - y)))

    def next_row(x, y):
        to = x + 1 if y < 2 else x - 1
        return (to, y) if 0 <= to < 4 else None

    across_row = send(across, chips(next_row))

    odd = y & 1
    has_above, has_below = x > 0, x < 3
    row_end = jnp.where(y == 0, has_above, jnp.where(y == 3, has_below, True))
    row_cross = jnp.where(y < 2, has_above, has_below)
    info = jnp.stack(
        [
            core ^ odd ^ 1,
            core ^ odd,
            jnp.int32(1),
            row_end.astype(jnp.int32),
            row_cross.astype(jnp.int32),
            has_above.astype(jnp.int32),
            has_below.astype(jnp.int32),
            core,
        ]
    ).astype(jnp.int32)
    mask = jnp.transpose(block_mask, (1, 2, 0))

    state = attend(info, mask, q, [local], [(0, False, 0, 2), (0, True, 1, 2)], None, None, False)
    state = attend(
        info,
        mask,
        q,
        [beside, across, above, below, far],
        [
            (0, False, 2, 2),
            (0, True, 1, 2),
            (1, False, 3, 2),
            (2, False, 4, 5),
            (3, False, 4, 6),
            (4, False, 5, 2),
        ],
        0,
        state,
        False,
    )
    state = attend(info, mask, q, [other], [(0, False, 2, 3), (0, True, 1, 3)], 1, state, False)
    attended = attend(info, mask, q, [across_row], [(0, False, 3, 4)], None, state, True)

    rows = lax.all_to_all(
        attended.reshape(FT // ROWS, 2 * ROWS, HD), ("core", "high"), 0, 0, tiled=True
    )
    pair = [(i, i ^ 2) for i in range(32)]
    low = lax.axis_index("low").reshape(1)
    far_rows = send(rows, pair)
    own, beside_z = product(low, rows, weight)
    got = lax.ppermute(beside_z, "low", [(0, 1), (1, 0)])
    far_rows, own = lax.optimization_barrier((far_rows, own))
    far, far_beside = product(low, far_rows, weight)
    far, got = lax.optimization_barrier((far, got))
    got_far = send(far, pair)
    both = [(2 * i + k, 2 * (i ^ 2) + (k ^ 1)) for i in range(32) for k in range(2)]
    got_far_other = lax.ppermute(far_beside, FRAMES + ("low",), both)
    return add_halves((y & 1).reshape(1), own, got, got_far, got_far_other)


def solution(mesh):
    devices = mesh.devices.reshape(4, 4, 2, 8, 2)
    mesh = jax.sharding.Mesh(devices, FRAMES + HEADS)
    split = P(FRAMES, HEADS)
    return jax.shard_map(
        shards,
        mesh=mesh,
        in_specs=(split, split, split, P(), P(HEADS, None)),
        out_specs=P(FRAMES + HEADS, None),
        check_vma=False,
    )
```

```python
import functools
import math

import jax
import jax.numpy as jnp
from jax import lax
from jax.experimental import pallas as pl
from jax.experimental.pallas import tpu as pltpu
from jax.sharding import PartitionSpec as P

HD = 128
BLK = 128
FT = 512
NB = 4
ROWS = 32
FRAMES = ("x", "y", "core")
HEADS = ("high", "low")
TILE = 256
CORE = 7
DOUT = 2560
HIDDEN = -1e30
SCALE = math.log2(math.e) / math.sqrt(HD)
VMEM = 40 * 1024 * 1024
NARROW = 24 * 1024 * 1024


def attend_kernel(sources, split, n_kv, first, last, *refs):
    info_ref, mask_ref, q_ref = refs[:3]
    kv_refs = refs[3 : 3 + n_kv]
    rest = refs[3 + n_kv :]
    state_in, outs = ((), rest) if first else (rest[:3], rest[3:])
    tiles = FT // TILE
    blocks = TILE // BLK

    def fold(frame, tile, seen):
        rows = pl.ds(pl.multiple_of(tile * TILE, TILE), TILE)
        q = q_ref[frame, rows, :]
        pieces = []
        for kv_no, cross, level, valid in seen:
            key_frame = 1 - frame if cross else frame
            scores = lax.dot_general(
                q,
                kv_refs[kv_no][2 * key_frame],
                (((1,), (1,)), ((), ())),
                preferred_element_type=jnp.float32,
            )
            here = info_ref[valid] > 0
            piece = []
            for a in range(blocks):
                row = []
                for b in range(NB):
                    shown = mask_ref[tile * blocks + a, b, level] > 0
                    bias = jnp.where(here & shown, jnp.float32(0.0), jnp.float32(HIDDEN))
                    block = scores[a * BLK : (a + 1) * BLK, b * BLK : (b + 1) * BLK]
                    row.append(block + bias)
                piece.append(row)
            pieces.append(piece)
        peaks, totals, accs, places = [], [], [], []
        for a in range(blocks):
            place = pl.ds(pl.multiple_of(tile * TILE + a * BLK, BLK), BLK)
            top = functools.reduce(jnp.maximum, [s for piece in pieces for s in piece[a]])
            peak = jnp.max(top, axis=1, keepdims=True)
            if first:
                peak = jnp.broadcast_to(peak, (BLK, BLK))
                totals.append(jnp.zeros((BLK, BLK), jnp.float32))
                accs.append(jnp.zeros((BLK, HD), jnp.float32))
            else:
                old = state_in[0][frame, place, :]
                peak = jnp.maximum(old, peak)
                shrink = jnp.exp2((old - peak) * SCALE)
                totals.append(state_in[1][frame, place, :] * shrink)
                accs.append(state_in[2][frame, place, :] * shrink)
            peaks.append(peak)
            places.append(place)
        acc = jnp.concatenate(accs, axis=0)
        for (kv_no, cross, _, _), piece in zip(seen, pieces):
            key_frame = 1 - frame if cross else frame
            packed = []
            for a in range(blocks):
                weights = [jnp.exp2((s - peaks[a]) * SCALE) for s in piece[a]]
                totals[a] = totals[a] + sum(weights)
                packed.append(
                    jnp.concatenate([w.astype(jnp.bfloat16) for w in weights], axis=1)
                )
            acc = acc + jnp.dot(
                jnp.concatenate(packed, axis=0),
                kv_refs[kv_no][2 * key_frame + 1],
                preferred_element_type=jnp.float32,
            )
        for a in range(blocks):
            part = acc[a * BLK : (a + 1) * BLK]
            if last:
                denom = jnp.sum(totals[a], axis=1, keepdims=True)
                attended = (part / denom).astype(jnp.bfloat16)
                chunk = (tile * blocks + a) * (BLK // ROWS)
                for i in range(BLK // ROWS):
                    outs[0][frame ^ info_ref[CORE], chunk + i] = attended[
                        i * ROWS : (i + 1) * ROWS
                    ]
            else:
                outs[0][frame, places[a], :] = peaks[a]
                outs[1][frame, places[a], :] = totals[a]
                outs[2][frame, places[a], :] = part

    alone = [source for source in sources if not source[1]]
    favoured = None if split is None else info_ref[split]

    @pl.loop(0, tiles)
    def _(tile):
        if split is None:
            fold(0, tile, sources)
            fold(1, tile, sources)
        else:
            fold(favoured, tile, sources)
            fold(1 - favoured, tile, alone)


def attend(info, mask, q, kvs, sources, split, state, last):
    first = state is None
    held = jax.ShapeDtypeStruct((2, FT, HD), jnp.float32)
    if last:
        out_shape = (jax.ShapeDtypeStruct((2, FT // ROWS, ROWS, HD), jnp.bfloat16),)
    else:
        out_shape = (held,) * 3
    vmem = pl.BlockSpec(memory_space=pltpu.VMEM)
    smem = pl.BlockSpec(memory_space=pltpu.SMEM)
    states = () if first else tuple(state)
    pairs = len(sources) * 2 - (split is not None)
    out = pl.pallas_call(
        functools.partial(attend_kernel, sources, split, len(kvs), first, last),
        out_shape=out_shape,
        in_specs=[smem, smem] + [vmem] * (1 + len(kvs) + len(states)),
        out_specs=(vmem,) * len(out_shape),
        compiler_params=pltpu.CompilerParams(vmem_limit_bytes=VMEM),
        cost_estimate=pl.CostEstimate(
            flops=pairs * 4 * FT * FT * HD,
            bytes_accessed=len(kvs) * 4 * FT * HD * 2,
            transcendentals=pairs * FT * FT,
        ),
    )(info, mask, q, *kvs, *states)
    return out[0] if last else out


def product_kernel(low_ref, rows_ref, w_ref, same_ref, other_ref, part_ref):
    rows = jnp.concatenate([rows_ref[n] for n in range(rows_ref.shape[0])], axis=1)
    part_ref[...] = jnp.dot(rows, w_ref[...], preferred_element_type=jnp.float32).astype(
        jnp.bfloat16
    )
    for k, out in enumerate((same_ref, other_ref)):
        start = pl.multiple_of((low_ref[0] ^ k) * ROWS, ROWS)
        out[...] = part_ref[pl.ds(start, ROWS), :]


def product(low, rows, weight):
    vmem = pl.BlockSpec(memory_space=pltpu.VMEM)
    depth, width = weight.shape
    part = jax.ShapeDtypeStruct((ROWS, width), weight.dtype)
    return pl.pallas_call(
        product_kernel,
        out_shape=(part,) * 2,
        in_specs=[pl.BlockSpec(memory_space=pltpu.SMEM)] + [vmem] * 2,
        out_specs=(vmem,) * 2,
        scratch_shapes=[pltpu.VMEM((2 * ROWS, width), weight.dtype)],
        compiler_params=pltpu.CompilerParams(vmem_limit_bytes=NARROW),
        cost_estimate=pl.CostEstimate(
            flops=4 * ROWS * depth * width, bytes_accessed=depth * width * 2, transcendentals=0
        ),
    )(low, rows, weight)


def add_kernel(side_ref, own_ref, got_ref, far_ref, far_other_ref, out_ref):
    width = own_ref.shape[1]
    side = side_ref[0]

    def add(place, left, right):
        both = left[...].astype(jnp.float32) + right[...].astype(jnp.float32)
        columns = pl.ds(pl.multiple_of(place * width, HD), width)
        out_ref[:, columns] = both.astype(jnp.bfloat16)

    add(side, own_ref, got_ref)
    add(1 - side, far_ref, far_other_ref)


def add_halves(side, own, got, far, far_other):
    vmem = pl.BlockSpec(memory_space=pltpu.VMEM)
    return pl.pallas_call(
        add_kernel,
        out_shape=jax.ShapeDtypeStruct((ROWS, 2 * own.shape[1]), own.dtype),
        in_specs=[pl.BlockSpec(memory_space=pltpu.SMEM)] + [vmem] * 4,
        out_specs=vmem,
        compiler_params=pltpu.CompilerParams(vmem_limit_bytes=NARROW),
    )(side, own, got, far, far_other)


def shards(queries, keys, values, block_mask, out_weight):
    me = lax.axis_index(FRAMES)
    core = me & 1
    y = (me >> 1) & 3
    x = me >> 3

    def chips(go):
        pairs = []
        for i in range(32):
            to = go(i // 8, (i // 2) % 4)
            if to is not None:
                pairs.append((i, to[0] * 8 + to[1] * 2 + i % 2))
        return pairs

    def send(array, pairs):
        return lax.ppermute(array, FRAMES, pairs)

    first_core, first_side = core == 0, (y & 1) == 0

    def corner(row, column):
        return out_weight[row * HD : (row + 1) * HD, column * half : (column + 1) * half]

    half = DOUT // 2
    weight = jnp.where(
        first_core,
        jnp.where(first_side, corner(0, 0), corner(0, 1)),
        jnp.where(first_side, corner(1, 0), corner(1, 1)),
    )
    weight, first_core = lax.optimization_barrier((weight, first_core))
    weight = lax.all_gather(weight, ("core", "high"), axis=0, tiled=True)

    def head(array, low):
        return jnp.where(low, array[:, :HD], array[:, HD:])

    swap = [(i, i ^ 1) for i in range(32)]
    given = jnp.stack([head(array, ~first_core) for array in (keys, values, queries)])
    got = send(given, swap)
    first_core, _ = lax.optimization_barrier((first_core, given))
    k_own, v_own, q_own = (head(array, first_core) for array in (keys, values, queries))
    local = jnp.concatenate([jnp.stack([k_own, v_own]), got[:2]], axis=0)
    q = jnp.concatenate([q_own[None], got[2:]], axis=0)

    across = send(local, chips(lambda x, y: (x, y ^ 2)))
    above = send(local, chips(lambda x, y: (x + 1, y) if x < 3 else None))
    below = send(local, chips(lambda x, y: (x - 1, y) if x > 0 else None))
    beside = send(local, chips(lambda x, y: (x, y ^ 1)))
    far = send(local, chips(lambda x, y: (x ^ 2, y)))
    turned = jnp.where((y == 1) | (y == 2), local, jnp.where(y == 3, above, below))
    other = send(turned, chips(lambda x, y: (x, 3 - y)))

    def next_row(x, y):
        to = x + 1 if y < 2 else x - 1
        return (to, y) if 0 <= to < 4 else None

    across_row = send(across, chips(next_row))

    odd = y & 1
    has_above, has_below = x > 0, x < 3
    row_end = jnp.where(y == 0, has_above, jnp.where(y == 3, has_below, True))
    row_cross = jnp.where(y < 2, has_above, has_below)
    info = jnp.stack(
        [
            core ^ odd ^ 1,
            core ^ odd,
            jnp.int32(1),
            row_end.astype(jnp.int32),
            row_cross.astype(jnp.int32),
            has_above.astype(jnp.int32),
            has_below.astype(jnp.int32),
            core,
        ]
    ).astype(jnp.int32)
    mask = jnp.transpose(block_mask, (1, 2, 0))

    state = attend(info, mask, q, [local], [(0, False, 0, 2), (0, True, 1, 2)], None, None, False)
    state = attend(
        info,
        mask,
        q,
        [across, above, below],
        [(0, False, 3, 2), (1, False, 4, 5), (2, False, 4, 6)],
        None,
        state,
        False,
    )
    state = attend(
        info,
        mask,
        q,
        [beside, far],
        [(0, False, 2, 2), (0, True, 1, 2), (1, False, 5, 2)],
        0,
        state,
        False,
    )
    state = attend(info, mask, q, [other], [(0, False, 2, 3), (0, True, 1, 3)], 1, state, False)
    attended = attend(info, mask, q, [across_row], [(0, False, 3, 4)], None, state, True)

    rows = lax.all_to_all(
        attended.reshape(FT // ROWS, 2 * ROWS, HD), ("core", "high"), 0, 0, tiled=True
    )
    pair = [(i, i ^ 2) for i in range(32)]
    low = lax.axis_index("low").reshape(1)
    far_rows = send(rows, pair)
    own, beside_z = product(low, rows, weight)
    got = lax.ppermute(beside_z, "low", [(0, 1), (1, 0)])
    far_rows, own = lax.optimization_barrier((far_rows, own))
    far, far_beside = product(low, far_rows, weight)
    far, got = lax.optimization_barrier((far, got))
    got_far = send(far, pair)
    both = [(2 * i + k, 2 * (i ^ 2) + (k ^ 1)) for i in range(32) for k in range(2)]
    got_far_other = lax.ppermute(far_beside, FRAMES + ("low",), both)
    return add_halves((y & 1).reshape(1), own, got, got_far, got_far_other)


def solution(mesh):
    devices = mesh.devices.reshape(4, 4, 2, 8, 2)
    mesh = jax.sharding.Mesh(devices, FRAMES + HEADS)
    split = P(FRAMES, HEADS)
    return jax.shard_map(
        shards,
        mesh=mesh,
        in_specs=(split, split, split, P(), P(HEADS, None)),
        out_specs=P(FRAMES + HEADS, None),
        check_vma=False,
    )
```

```python
import functools
import math

import jax
import jax.numpy as jnp
from jax import lax
from jax.experimental import pallas as pl
from jax.experimental.pallas import tpu as pltpu
from jax.sharding import PartitionSpec as P

HD = 128
BLK = 128
FT = 512
NB = 4
ROWS = 32
FRAMES = ("x", "y", "core")
HEADS = ("high", "low")
TILE = 256
CORE = 7
DOUT = 2560
HIDDEN = -1e30
SCALE = math.log2(math.e) / math.sqrt(HD)
VMEM = 40 * 1024 * 1024
NARROW = 24 * 1024 * 1024


def attend_kernel(sources, split, n_kv, first, last, *refs):
    info_ref, mask_ref, q_ref = refs[:3]
    kv_refs = refs[3 : 3 + n_kv]
    rest = refs[3 + n_kv :]
    state_in, outs = ((), rest) if first else (rest[:3], rest[3:])
    tiles = FT // TILE
    blocks = TILE // BLK

    def fold(frame, tile, seen):
        rows = pl.ds(pl.multiple_of(tile * TILE, TILE), TILE)
        q = q_ref[frame, rows, :]
        pieces = []
        for kv_no, cross, level, valid in seen:
            key_frame = 1 - frame if cross else frame
            scores = lax.dot_general(
                q,
                kv_refs[kv_no][2 * key_frame],
                (((1,), (1,)), ((), ())),
                preferred_element_type=jnp.float32,
            )
            here = info_ref[valid] > 0
            piece = []
            for a in range(blocks):
                row = []
                for b in range(NB):
                    shown = mask_ref[tile * blocks + a, b, level] > 0
                    bias = jnp.where(here & shown, jnp.float32(0.0), jnp.float32(HIDDEN))
                    block = scores[a * BLK : (a + 1) * BLK, b * BLK : (b + 1) * BLK]
                    row.append(block + bias)
                piece.append(row)
            pieces.append(piece)
        peaks, totals, accs, places = [], [], [], []
        for a in range(blocks):
            place = pl.ds(pl.multiple_of(tile * TILE + a * BLK, BLK), BLK)
            top = functools.reduce(jnp.maximum, [s for piece in pieces for s in piece[a]])
            peak = jnp.max(top, axis=1, keepdims=True)
            if first:
                peak = jnp.broadcast_to(peak, (BLK, BLK))
                totals.append(jnp.zeros((BLK, BLK), jnp.float32))
                accs.append(jnp.zeros((BLK, HD), jnp.float32))
            else:
                old = state_in[0][frame, place, :]
                peak = jnp.maximum(old, peak)
                shrink = jnp.exp2((old - peak) * SCALE)
                totals.append(state_in[1][frame, place, :] * shrink)
                accs.append(state_in[2][frame, place, :] * shrink)
            peaks.append(peak)
            places.append(place)
        acc = jnp.concatenate(accs, axis=0)
        for (kv_no, cross, _, _), piece in zip(seen, pieces):
            key_frame = 1 - frame if cross else frame
            packed = []
            for a in range(blocks):
                weights = [jnp.exp2((s - peaks[a]) * SCALE) for s in piece[a]]
                totals[a] = totals[a] + sum(weights)
                packed.append(
                    jnp.concatenate([w.astype(jnp.bfloat16) for w in weights], axis=1)
                )
            acc = acc + jnp.dot(
                jnp.concatenate(packed, axis=0),
                kv_refs[kv_no][2 * key_frame + 1],
                preferred_element_type=jnp.float32,
            )
        for a in range(blocks):
            part = acc[a * BLK : (a + 1) * BLK]
            if last:
                denom = jnp.sum(totals[a], axis=1, keepdims=True)
                attended = (part / denom).astype(jnp.bfloat16)
                chunk = (tile * blocks + a) * (BLK // ROWS)
                for i in range(BLK // ROWS):
                    outs[0][frame ^ info_ref[CORE], chunk + i] = attended[
                        i * ROWS : (i + 1) * ROWS
                    ]
            else:
                outs[0][frame, places[a], :] = peaks[a]
                outs[1][frame, places[a], :] = totals[a]
                outs[2][frame, places[a], :] = part

    alone = [source for source in sources if not source[1]]
    favoured = None if split is None else info_ref[split]

    @pl.loop(0, tiles)
    def _(tile):
        if split is None:
            fold(0, tile, sources)
            fold(1, tile, sources)
        else:
            fold(favoured, tile, sources)
            fold(1 - favoured, tile, alone)


def attend(info, mask, q, kvs, sources, split, state, last):
    first = state is None
    held = jax.ShapeDtypeStruct((2, FT, HD), jnp.float32)
    if last:
        out_shape = (jax.ShapeDtypeStruct((2, FT // ROWS, ROWS, HD), jnp.bfloat16),)
    else:
        out_shape = (held,) * 3
    vmem = pl.BlockSpec(memory_space=pltpu.VMEM)
    smem = pl.BlockSpec(memory_space=pltpu.SMEM)
    states = () if first else tuple(state)
    pairs = len(sources) * 2 - (split is not None)
    out = pl.pallas_call(
        functools.partial(attend_kernel, sources, split, len(kvs), first, last),
        out_shape=out_shape,
        in_specs=[smem, smem] + [vmem] * (1 + len(kvs) + len(states)),
        out_specs=(vmem,) * len(out_shape),
        compiler_params=pltpu.CompilerParams(vmem_limit_bytes=VMEM),
        cost_estimate=pl.CostEstimate(
            flops=pairs * 4 * FT * FT * HD,
            bytes_accessed=len(kvs) * 4 * FT * HD * 2,
            transcendentals=pairs * FT * FT,
        ),
    )(info, mask, q, *kvs, *states)
    return out[0] if last else out


def product_kernel(low_ref, rows_ref, w_ref, same_ref, other_ref, part_ref):
    rows = jnp.concatenate([rows_ref[n] for n in range(rows_ref.shape[0])], axis=1)
    part_ref[...] = jnp.dot(rows, w_ref[...], preferred_element_type=jnp.float32).astype(
        jnp.bfloat16
    )
    for k, out in enumerate((same_ref, other_ref)):
        start = pl.multiple_of((low_ref[0] ^ k) * ROWS, ROWS)
        out[...] = part_ref[pl.ds(start, ROWS), :]


def product(low, rows, weight):
    vmem = pl.BlockSpec(memory_space=pltpu.VMEM)
    depth, width = weight.shape
    part = jax.ShapeDtypeStruct((ROWS, width), weight.dtype)
    return pl.pallas_call(
        product_kernel,
        out_shape=(part,) * 2,
        in_specs=[pl.BlockSpec(memory_space=pltpu.SMEM)] + [vmem] * 2,
        out_specs=(vmem,) * 2,
        scratch_shapes=[pltpu.VMEM((2 * ROWS, width), weight.dtype)],
        compiler_params=pltpu.CompilerParams(vmem_limit_bytes=NARROW),
        cost_estimate=pl.CostEstimate(
            flops=4 * ROWS * depth * width, bytes_accessed=depth * width * 2, transcendentals=0
        ),
    )(low, rows, weight)


def add_kernel(side_ref, own_ref, got_ref, far_ref, far_other_ref, out_ref):
    width = own_ref.shape[1]
    side = side_ref[0]

    def add(place, left, right):
        both = left[...].astype(jnp.float32) + right[...].astype(jnp.float32)
        columns = pl.ds(pl.multiple_of(place * width, HD), width)
        out_ref[:, columns] = both.astype(jnp.bfloat16)

    add(side, own_ref, got_ref)
    add(1 - side, far_ref, far_other_ref)


def add_halves(side, own, got, far, far_other):
    vmem = pl.BlockSpec(memory_space=pltpu.VMEM)
    return pl.pallas_call(
        add_kernel,
        out_shape=jax.ShapeDtypeStruct((ROWS, 2 * own.shape[1]), own.dtype),
        in_specs=[pl.BlockSpec(memory_space=pltpu.SMEM)] + [vmem] * 4,
        out_specs=vmem,
        compiler_params=pltpu.CompilerParams(vmem_limit_bytes=NARROW),
    )(side, own, got, far, far_other)


def shards(queries, keys, values, block_mask, out_weight):
    me = lax.axis_index(FRAMES)
    core = me & 1
    y = (me >> 1) & 3
    x = me >> 3

    def chips(go):
        pairs = []
        for i in range(32):
            to = go(i // 8, (i // 2) % 4)
            if to is not None:
                pairs.append((i, to[0] * 8 + to[1] * 2 + i % 2))
        return pairs

    def send(array, pairs):
        return lax.ppermute(array, FRAMES, pairs)

    first_core, half = core == 0, DOUT // 2
    weight = lax.dynamic_slice_in_dim(out_weight, core * HD, HD, 0)
    weight = jnp.where((y & 1) == 0, weight[:, :half], weight[:, half:])
    weight, first_core = lax.optimization_barrier((weight, first_core))
    weight = lax.all_gather(weight, ("core", "high"), axis=0, tiled=True)

    def head(array, low):
        return jnp.where(low, array[:, :HD], array[:, HD:])

    swap = [(i, i ^ 1) for i in range(32)]
    given = jnp.stack([head(array, ~first_core) for array in (keys, values, queries)])
    got = send(given, swap)
    first_core, _ = lax.optimization_barrier((first_core, given))
    k_own, v_own, q_own = (head(array, first_core) for array in (keys, values, queries))
    local = jnp.concatenate([jnp.stack([k_own, v_own]), got[:2]], axis=0)
    q = jnp.concatenate([q_own[None], got[2:]], axis=0)

    across = send(local, chips(lambda x, y: (x, y ^ 2)))
    above = send(local, chips(lambda x, y: (x + 1, y) if x < 3 else None))
    below = send(local, chips(lambda x, y: (x - 1, y) if x > 0 else None))
    beside = send(local, chips(lambda x, y: (x, y ^ 1)))
    far = send(local, chips(lambda x, y: (x ^ 2, y)))
    turned = jnp.where((y == 1) | (y == 2), local, jnp.where(y == 3, above, below))
    other = send(turned, chips(lambda x, y: (x, 3 - y)))

    def next_row(x, y):
        to = x + 1 if y < 2 else x - 1
        return (to, y) if 0 <= to < 4 else None

    across_row = send(across, chips(next_row))

    odd = y & 1
    has_above, has_below = x > 0, x < 3
    row_end = jnp.where(y == 0, has_above, jnp.where(y == 3, has_below, True))
    row_cross = jnp.where(y < 2, has_above, has_below)
    info = jnp.stack(
        [
            core ^ odd ^ 1,
            core ^ odd,
            jnp.int32(1),
            row_end.astype(jnp.int32),
            row_cross.astype(jnp.int32),
            has_above.astype(jnp.int32),
            has_below.astype(jnp.int32),
            core,
        ]
    ).astype(jnp.int32)
    mask = jnp.transpose(block_mask, (1, 2, 0))

    state = attend(info, mask, q, [local], [(0, False, 0, 2), (0, True, 1, 2)], None, None, False)
    state = attend(
        info,
        mask,
        q,
        [across, above, below],
        [(0, False, 3, 2), (1, False, 4, 5), (2, False, 4, 6)],
        None,
        state,
        False,
    )
    state = attend(
        info,
        mask,
        q,
        [beside, far],
        [(0, False, 2, 2), (0, True, 1, 2), (1, False, 5, 2)],
        0,
        state,
        False,
    )
    state = attend(info, mask, q, [other], [(0, False, 2, 3), (0, True, 1, 3)], 1, state, False)
    attended = attend(info, mask, q, [across_row], [(0, False, 3, 4)], None, state, True)

    rows = lax.all_to_all(
        attended.reshape(FT // ROWS, 2 * ROWS, HD), ("core", "high"), 0, 0, tiled=True
    )
    pair = [(i, i ^ 2) for i in range(32)]
    low = lax.axis_index("low").reshape(1)
    far_rows = send(rows, pair)
    own, beside_z = product(low, rows, weight)
    got = lax.ppermute(beside_z, "low", [(0, 1), (1, 0)])
    far_rows, own = lax.optimization_barrier((far_rows, own))
    far, far_beside = product(low, far_rows, weight)
    far, got = lax.optimization_barrier((far, got))
    got_far = send(far, pair)
    both = [(2 * i + k, 2 * (i ^ 2) + (k ^ 1)) for i in range(32) for k in range(2)]
    got_far_other = lax.ppermute(far_beside, FRAMES + ("low",), both)
    return add_halves((y & 1).reshape(1), own, got, got_far, got_far_other)


def solution(mesh):
    devices = mesh.devices.reshape(4, 4, 2, 8, 2)
    mesh = jax.sharding.Mesh(devices, FRAMES + HEADS)
    split = P(FRAMES, HEADS)
    return jax.shard_map(
        shards,
        mesh=mesh,
        in_specs=(split, split, split, P(), P(HEADS, None)),
        out_specs=P(FRAMES + HEADS, None),
        check_vma=False,
    )
```
